256 devices in a mesh: sfc: 16 (over x, y), sub: 16 (over z, core).
Axes of the slice: x: 4, y: 4, z: 8, core: 2. Of those that a mesh axis runs over, the one named last changes fastest.
Arguments:
- pot_temp: float32 [8192, 16, 128], P(('sfc', 'sub')), may hold values from -6 to 6
- tracer: float32 [8192, 16, 128], P(('sfc', 'sub')), may hold values from -6 to 6
- wind_u: float32 [8192, 16, 128], P(('sfc', 'sub')), may hold values from -6 to 6
- wind_v: float32 [8192, 16, 128], P(('sfc', 'sub')), may hold values from -6 to 6
- vert_w: float32 [8192, 16, 128], P(('sfc', 'sub')), may hold values from -6 to 6
- geopot: float32 [8192, 16, 128], P(('sfc', 'sub')), may hold values from -6 to 6
- elem_mass: float32 [8192, 16], P(('sfc', 'sub')), may hold values from 0.25 to 4
- deriv_x: float32 [16, 16], replicated, may hold values from -1.5 to 1.5
- deriv_y: float32 [16, 16], replicated, may hold values from -1.5 to 1.5
- col_inverse: float32 [128, 128], replicated, may hold values from 0 to 1, as said below
- element_cell: int32 [256, 32], P(('sfc', 'sub')), may hold values from 0 to 31, each once within a row
Outputs:
- temp_out: float32 [8192, 16, 128], P(('sfc', 'sub'))
- tracer_out: float32 [8192, 16, 128], P(('sfc', 'sub'))
- wind_u_out: float32 [8192, 16, 128], P(('sfc', 'sub'))
- wind_v_out: float32 [8192, 16, 128], P(('sfc', 'sub'))
- vert_w_out: float32 [8192, 16, 128], P(('sfc', 'sub'))
- geopot_out: float32 [8192, 16, 128], P(('sfc', 'sub'))
The draws below stay inside these ranges and needn't reach their ends.
Inputs may be any that keep to these rules, and one draw needn't show every extreme that they name: `element_cell`: each device's row names every cell of its tile once. `col_inverse`: an approximate inverse of the derivative of r at a reference column state: symmetric, with positive entries.
All inputs are finite; a program needn't handle non-finite values.
Results may differ from the reference program's by a relative error of at most 0.0001.
Values sent between devices are 32-bit elements; how exact they have to be, the bound alone decides.
A program may use at most 64 MiB of HBM per device.

```python
import math
import jax
import jax.numpy as jnp
from jax import lax

LEV = 128
GLL = 16
TX = 4
TY = 8
NEWTON = 3
ELEM_DEV = 32
DEVS = 256
ELEMS = 8192
N_SFC = 16
N_SUB = 16


def closed_inverse(slopes, decay):
    below = jnp.concatenate([jnp.zeros((1,), jnp.float32), slopes[:-1]])
    diag_scale = 1.0 / jnp.sqrt(1.0 + 0.25 * (slopes + below))
    levels = jnp.arange(LEV, dtype=jnp.float32)
    distance = jnp.abs(levels[:, None] - levels[None, :])
    falloff = jnp.exp(distance * jnp.log(decay))
    return (diag_scale[:, None] * diag_scale[None, :] * falloff).astype(jnp.float32)


def draw_col_inverse(key, part):
    key = jax.random.fold_in(key, 7)
    slope_key = jax.random.fold_in(key, 1)
    decay_key = jax.random.fold_in(key, 2)
    slopes = jax.random.uniform(slope_key, (LEV,), jnp.float32, 0.2, 1.0)
    decay = jax.random.uniform(decay_key, (), jnp.float32, 0.12, 0.25)
    return closed_inverse(slopes, decay)


def shard_levels(key, extent, cuts, low, high):
    loudness = 1.0
    for dim, blocks in cuts:
        heights = jax.random.uniform(jax.random.fold_in(jax.random.fold_in(key, 6), dim), (blocks,), jnp.float32, low / len(cuts), high / len(cuts))
        loudness = loudness * jnp.repeat(jnp.exp(heights), extent[dim] // blocks).reshape((-1,) + (1,) * (len(extent) - 1 - dim))
    return loudness


def centred(rng, dims, spread, bound, cuts=(), held_as=jnp.bfloat16):
    level = shard_levels(rng, dims, cuts, -0.22, 0.18) if cuts else 1.0
    array = jax.random.normal(rng, dims, jnp.float32) * spread * level
    return jnp.minimum(jnp.maximum(array, -bound), bound).astype(held_as)


def setup_inputs(seed: int = 0) -> dict:
    key_of = jax.random.split(jax.random.key(seed), 12)
    pot_temp = centred(key_of[0], (ELEMS, GLL, LEV), 1.0, 6.0, ((0, 256),), jnp.float32)
    tracer = centred(key_of[1], (ELEMS, GLL, LEV), 1.0, 6.0, ((0, 256),), jnp.float32)
    wind_u = centred(key_of[2], (ELEMS, GLL, LEV), 1.0, 6.0, ((0, 256),), jnp.float32)
    wind_v = centred(key_of[3], (ELEMS, GLL, LEV), 1.0, 6.0, ((0, 256),), jnp.float32)
    vert_w = centred(key_of[4], (ELEMS, GLL, LEV), 1.0, 6.0, ((0, 256),), jnp.float32)
    geopot = centred(key_of[5], (ELEMS, GLL, LEV), 1.0, 6.0, ((0, 256),), jnp.float32)
    elem_mass = jnp.clip(jnp.exp(math.log(4.0) - 2.7725887 * jax.random.uniform(key_of[6], (ELEMS, GLL), jnp.float32) ** shard_levels(key_of[6], (ELEMS, GLL), ((0, 256),), -0.2, 0.2)), 0.25, 4.0)
    deriv_x = centred(key_of[7], (GLL, GLL), GLL ** -0.5, 1.5, (), jnp.float32)
    deriv_y = centred(key_of[8], (GLL, GLL), GLL ** -0.5, 1.5, (), jnp.float32)
    col_inverse = draw_col_inverse(jax.random.fold_in(key_of[11], 71), 0)
    element_cell = jax.vmap(lambda own: jax.random.permutation(own, ELEM_DEV))(jax.random.split(key_of[10], DEVS)).reshape((DEVS, ELEM_DEV)).astype(jnp.int32)
    return dict(pot_temp=pot_temp, tracer=tracer, wind_u=wind_u, wind_v=wind_v, vert_w=vert_w, geopot=geopot, elem_mass=elem_mass, deriv_x=deriv_x, deriv_y=deriv_y, col_inverse=col_inverse, element_cell=element_cell)


time_step = 0.4
visc_coef = 0.1
buoyancy = 0.5
gravity_step = 0.5
column_couple = 0.25


def global_nodes(element_cell):
    device_ids = jnp.arange(element_cell.shape[0], dtype=jnp.int32)
    tile_row = device_ids // N_SUB
    tile_col = device_ids % N_SUB
    elem_row = tile_row[:, None] * TY + element_cell // TX
    elem_col = tile_col[:, None] * TX + element_cell % TX
    points = jnp.arange(16, dtype=jnp.int32)
    grid_rows = 3 * TY * N_SFC
    grid_cols = 3 * TX * N_SUB
    node_row = (elem_row[:, :, None] * 3 + points // 4) % grid_rows
    node_col = (elem_col[:, :, None] * 3 + points % 4) % grid_cols
    return (node_row * grid_cols + node_col).reshape(-1).astype(jnp.int32), grid_rows * grid_cols


def derive(matrix, field):
    return jnp.einsum("ij,ejl->eil", matrix, field, precision=lax.Precision.HIGHEST)


def laplace(deriv_x, deriv_y, field):
    return derive(deriv_x, derive(deriv_x, field)) + derive(deriv_y, derive(deriv_y, field))


def column_residual(phi, target):
    phi_above = jnp.concatenate([phi[..., 1:], jnp.zeros_like(phi[..., :1])], axis=-1)
    flux_here = jnp.tanh(phi_above - phi)
    flux_below = jnp.concatenate([jnp.zeros_like(flux_here[..., :1]), flux_here[..., :-1]], axis=-1)
    return phi - target - column_couple * (flux_here - flux_below)


def reference(pot_temp, tracer, wind_u, wind_v, vert_w, geopot, elem_mass, deriv_x, deriv_y, col_inverse, element_cell):
    node_ids, node_count = global_nodes(element_cell)
    mass_sum = jax.ops.segment_sum(elem_mass.reshape(-1), node_ids, num_segments=node_count)[node_ids]

    def average(field):
        flattened = (field * elem_mass[:, :, None]).reshape(-1, field.shape[2])
        node_sums = jax.ops.segment_sum(flattened, node_ids, num_segments=node_count)[node_ids]
        return (node_sums / mass_sum[:, None]).reshape(field.shape)

    tend_temp = -(wind_u * derive(deriv_x, pot_temp) + wind_v * derive(deriv_y, pot_temp))
    tend_tracer = -(wind_u * derive(deriv_x, tracer) + wind_v * derive(deriv_y, tracer))
    tend_u = -derive(deriv_x, geopot)
    tend_v = -derive(deriv_y, geopot)
    tend_w = -(wind_u * derive(deriv_x, vert_w) + wind_v * derive(deriv_y, vert_w)) + buoyancy * pot_temp
    states = [pot_temp, tracer, wind_u, wind_v, vert_w]
    tendencies = [tend_temp, tend_tracer, tend_u, tend_v, tend_w]
    middle = [state + time_step * average(change) for state, change in zip(states, tendencies)]
    finals = []
    for field_idx in range(4):
        smooth = average(laplace(deriv_x, deriv_y, middle[field_idx]))
        smooth = average(laplace(deriv_x, deriv_y, smooth))
        finals.append(middle[field_idx] - visc_coef * smooth)
    target = geopot + gravity_step * middle[4]
    phi = target
    for newton_idx in range(NEWTON):
        resid = column_residual(phi, target)
        step_size = jnp.dot(resid.reshape(-1, resid.shape[-1]), col_inverse, precision=lax.Precision.HIGHEST)
        phi = phi - step_size.reshape(phi.shape)
    new_w = (phi - geopot) / gravity_step
    return finals[0], finals[1], finals[2], finals[3], new_w, phi
```

```python
import jax
import jax.numpy as jnp
from jax import lax
from jax.experimental import pallas as pl
from jax.experimental.pallas import tpu as pltpu
from jax.sharding import PartitionSpec as P

TX = 4
TY = 8
LEV = 128
NEWTON = 3
PITCH = 16
ROWS = 3 * TY + 1
NODES = ROWS * PITCH
STRIP = 64
FIELDS = 6

time_step = 0.4
visc_coef = 0.1
buoyancy = 0.5
gravity_step = 0.5
column_couple = 0.25

F32 = jnp.float32
BF16 = jnp.bfloat16
MESH = pl.DeviceIdType.MESH

SIDES = ((0, -1), (0, 1), (-1, 0), (1, 0), (-1, -1), (-1, 1), (1, -1), (1, 1))
OPPOSITE = (1, 0, 3, 2, 7, 6, 5, 4)
OFFSET = (0, 32, 64, 80, 96, 104, 112, 120)
COUNT = (32, 32, 16, 16, 8, 8, 8, 8)
CORNER_NODE = (0, 12, NODES - PITCH, NODES - PITCH + 12)


def iota(shape, dim):
    return lax.broadcasted_iota(jnp.int32, shape, dim)


def halves(x):
    high = x.astype(BF16)
    return high, (x - high.astype(F32)).astype(BF16)


def stack2(x):
    high, low = halves(x)
    return jnp.concatenate([high, low], axis=0)


def stack3(x):
    high, low = halves(x)
    return jnp.concatenate([high, low, high], axis=0)


def weight3(x):
    high, low = halves(x)
    return jnp.where(iota(x.shape, 1) < 2 * (x.shape[1] // 3), high.astype(F32), low.astype(F32)).astype(BF16)


def mm(a, b):
    return jnp.dot(a, b, preferred_element_type=F32)


def exact(a, b):
    return jnp.dot(a, b, preferred_element_type=F32, precision=lax.Precision.HIGHEST)


def onehot(cond):
    return jnp.where(cond, 1.0, 0.0).astype(F32)


def block_diag(matrix, cols):
    left = onehot(iota((STRIP, 16), 0) % 16 == iota((STRIP, 16), 1))
    right = onehot(iota((16, cols), 1) % 16 == iota((16, cols), 0))
    spread = exact(exact(left, matrix), right)
    same = (iota((STRIP, cols), 1) % STRIP) // 16 == iota((STRIP, cols), 0) // 16
    return jnp.where(same, spread, 0.0)


def node_point(node, point):
    return (node // PITCH == (point % 16) // 4) & (node % PITCH == 3 * (point // 16) + point % 4)


def gather_rim(grid, send):
    for k in range(grid.shape[0]):
        send[k, 0:ROWS] = grid[k, pl.ds(0, ROWS, stride=PITCH)]
        send[k, 32 : 32 + ROWS] = grid[k, pl.ds(12, ROWS, stride=PITCH)]
        send[k, 64:80] = grid[k, 0:16]
        send[k, 80:96] = grid[k, NODES - 16 : NODES]
        for corner, node in enumerate(CORNER_NODE):
            send[k, 96 + 8 * corner : 97 + 8 * corner] = grid[k, node : node + 1]


def add_rim(grid, recv):
    for k in range(grid.shape[0]):
        for first, rows in ((0, pl.ds(0, ROWS, stride=PITCH)), (32, pl.ds(12, ROWS, stride=PITCH))):
            grid[k, rows] = grid[k, rows] + recv[k, first : first + ROWS]
        grid[k, 0:16] = grid[k, 0:16] + recv[k, 64:80]
        grid[k, NODES - 16 : NODES] = grid[k, NODES - 16 : NODES] + recv[k, 80:96]
        for corner, node in enumerate(CORNER_NODE):
            grid[k, node : node + 1] = grid[k, node : node + 1] + recv[k, 96 + 8 * corner : 97 + 8 * corner]


def step_kernel(
    pot_in, tracer_in, u_in, v_in, w_in, geo_in, mass_in, dx_in, dy_in, col_in, cells, cells_row,
    out,
    xin, xc, mid, s1, s2, s3, mgrid, rinv, mcol, kmat, inv,
    send0, recv0, send1, recv1, send2, recv2, send3, recv3,
    load_sem, send_sem, recv_sem,
):
    row = lax.axis_index("sfc")
    col = lax.axis_index("sub")
    n_row = lax.axis_size("sfc")
    n_col = lax.axis_size("sub")

    def device(side):
        return (lax.rem(row + side[0] + n_row, n_row), lax.rem(col + side[1] + n_col, n_col))

    barrier = pltpu.get_barrier_semaphore()
    for side in SIDES:
        pl.semaphore_signal(barrier, inc=1, device_id=device(side), device_id_type=MESH)

    sources = (geo_in, w_in, pot_in, tracer_in, u_in, v_in)
    loads = [pltpu.make_async_copy(ref, xin.at[k], load_sem.at[k]) for k, ref in enumerate(sources)]
    for load in loads:
        load.start()

    def exchange(turn, send, recv):
        copies = []
        for k in range(8):
            copies.append(
                pltpu.make_async_remote_copy(
                    src_ref=send.at[:, pl.ds(OFFSET[k], COUNT[k])],
                    dst_ref=recv.at[:, pl.ds(OFFSET[OPPOSITE[k]], COUNT[k])],
                    send_sem=send_sem.at[turn, k],
                    recv_sem=recv_sem.at[turn, OPPOSITE[k]],
                    device_id=device(SIDES[k]),
                    device_id_type=MESH,
                )
            )
        return copies

    def invert(c, carry):
        slot = jnp.int32(0)
        for j in range(TX * TY):
            slot = jnp.where(cells[0, j] == c, j, slot)
        inv[c] = slot
        return carry

    lax.fori_loop(0, TX * TY, invert, 0)

    dx = dx_in[...]
    dy = dy_in[...]
    lap = exact(dx, dx) + exact(dy, dy)
    lap_blk = block_diag(lap, 3 * STRIP)
    deriv3 = weight3(jnp.concatenate([block_diag(dx, 3 * STRIP), block_diag(dy, 3 * STRIP)], axis=0))
    spread3 = onehot(node_point(iota((STRIP, 3 * STRIP), 1) % STRIP, iota((STRIP, 3 * STRIP), 0)))
    lap_nodes = exact(block_diag(lap, STRIP), spread3)
    gather2 = onehot(node_point(iota((STRIP, 2 * STRIP), 0), iota((STRIP, 2 * STRIP), 1) % STRIP)).astype(BF16)
    spread2 = onehot(node_point(iota((STRIP, 2 * STRIP), 1) % STRIP, iota((STRIP, 2 * STRIP), 0))).astype(BF16)

    for send in (send0, send1, send2, send3):
        send[...] = jnp.zeros_like(send)
    for grid in (s1, s2, s3, mgrid):
        grid[:, 0:16] = jnp.zeros((grid.shape[0], 16, LEV), F32)

    def accumulate(grid, start, vals):
        head = pl.ds(start, 16)
        tail = pl.ds(pl.multiple_of(start + 16, 16), STRIP - 16)
        for k in range(grid.shape[0]):
            part = vals[:, k * LEV : (k + 1) * LEV]
            grid[k, head] = grid[k, head] + part[0:16]
            grid[k, tail] = part[16:]

    def scaled_strip(grid, here, inverse, count):
        return jnp.concatenate([grid[k, here] * inverse for k in range(count)], axis=1)

    def mass_strip(ey, carry):
        points = []
        for ex in range(TX):
            chosen = jnp.where(cells_row[...] == TX * ey + ex, mass_in[...], 0.0)
            points.append(jnp.broadcast_to(jnp.sum(chosen, axis=1, keepdims=True), (16, LEV)))
        strip_mass = jnp.concatenate(points, axis=0)
        mcol[pl.ds(pl.multiple_of(STRIP * ey, STRIP), STRIP)] = strip_mass
        accumulate(mgrid, pl.multiple_of(48 * ey, 16), mm(gather2, stack2(strip_mass)))
        wide = jnp.concatenate([strip_mass, strip_mass[:, :STRIP]], axis=1)
        kmat[0, ey] = weight3(mm(gather2, stack2(wide * lap_blk)))
        kmat[1, ey] = weight3(mm(gather2, stack2(wide * lap_nodes)))
        return carry

    lax.fori_loop(0, TY, mass_strip, 0)
    gather_rim(mgrid, send0)
    pl.semaphore_wait(barrier, 8)
    mass_copies = exchange(0, send0, recv0)
    for copy in mass_copies:
        copy.start()

    for load in loads:
        load.wait()

    def strip_of(ref, ey, fields):
        return jnp.concatenate([ref[k, pl.ds(TX * ey, TX)].reshape(STRIP, LEV) for k in fields], axis=1)

    def tend_strip(ey, carry):
        points = pl.ds(pl.multiple_of(STRIP * ey, STRIP), STRIP)
        for ex in range(TX):
            slot = inv[TX * ey + ex]
            for k in range(FIELDS):
                xc[k, TX * ey + ex] = xin[k, slot]
        x = strip_of(xc, ey, range(FIELDS))
        x3 = stack3(x)
        slopes = mm(deriv3, x3[:, : 4 * LEV])
        sx = slopes[:STRIP]
        sy = slopes[STRIP:]
        pot = x[:, 2 * LEV : 3 * LEV]
        u = x[:, 4 * LEV : 5 * LEV]
        v = x[:, 5 * LEV : 6 * LEV]

        def advect(k):
            cols = slice(k * LEV, (k + 1) * LEV)
            return -(u * sx[:, cols] + v * sy[:, cols])

        tend = [advect(2), advect(3), -sx[:, :LEV], -sy[:, :LEV], advect(1) + buoyancy * pot]
        weight = mcol[points]
        weighted = jnp.concatenate([t * weight for t in tend], axis=1)
        start = pl.multiple_of(48 * ey, 16)
        accumulate(s1, start, mm(gather2, stack2(weighted)))
        accumulate(s2, start, mm(kmat[0, ey], x3[:, 2 * LEV :]))
        return carry

    lax.fori_loop(0, TY, tend_strip, 0)
    gather_rim(s1, send1)
    tend_copies = exchange(1, send1, recv1)
    for copy in tend_copies:
        copy.start()

    for copy in mass_copies:
        copy.wait()
    add_rim(mgrid, recv0)
    total_mass = mgrid[0]
    rinv[...] = jnp.where(total_mass > 0.0, 1.0 / jnp.where(total_mass > 0.0, total_mass, 1.0), 0.0)

    for copy in tend_copies:
        copy.wait()
    add_rim(s1, recv1)

    def lap_strip(source, scale):
        def body(ey, carry):
            start = pl.multiple_of(48 * ey, 16)
            here = pl.ds(start, STRIP)
            inverse = rinv[here] * scale
            nodal = scaled_strip(source, here, inverse, 4)
            vals = mm(kmat[1, ey], stack3(nodal))
            if source is s1:
                for k in range(4):
                    s2[k, here] = s2[k, here] + vals[:, k * LEV : (k + 1) * LEV]
            else:
                accumulate(s3, start, vals)
            return carry

        return body

    lax.fori_loop(0, TY, lap_strip(s1, time_step), 0)
    gather_rim(s2, send2)
    first_copies = exchange(2, send2, recv2)
    for copy in first_copies:
        copy.start()

    def mid_strip(ey, carry):
        here = pl.ds(pl.multiple_of(48 * ey, 16), STRIP)
        inverse = rinv[here] * time_step
        nodal = scaled_strip(s1, here, inverse, 5)
        change = mm(spread2, stack2(nodal))
        state = strip_of(xc, ey, (2, 3, 4, 5, 1)) + change
        for k in range(5):
            mid[k, pl.ds(TX * ey, TX)] = state[:, k * LEV : (k + 1) * LEV].reshape(TX, 16, LEV)
        return carry

    lax.fori_loop(0, TY, mid_strip, 0)

    for copy in first_copies:
        copy.wait()
    add_rim(s2, recv2)
    lax.fori_loop(0, TY, lap_strip(s2, 1.0), 0)
    gather_rim(s3, send3)
    second_copies = exchange(3, send3, recv3)
    for copy in second_copies:
        copy.start()

    col_high, col_low = halves(col_in[...])
    col3 = jnp.concatenate([col_high, col_high, col_low], axis=0)
    lane = iota((128, LEV), 1)

    def newton_rows(part, carry):
        elems = pl.ds(8 * part, 8)
        geo = xc[0, elems].reshape(128, LEV)
        target = geo + gravity_step * mid[4, elems].reshape(128, LEV)
        phi = target
        for _ in range(NEWTON):
            above = jnp.where(lane == LEV - 1, 0.0, pltpu.roll(phi, LEV - 1, 1))
            flux = jnp.tanh(above - phi)
            below = jnp.where(lane == 0, 0.0, pltpu.roll(flux, 1, 1))
            resid = phi - target - column_couple * (flux - below)
            high, low = halves(resid)
            phi = phi - mm(jnp.concatenate([high, low, high], axis=1), col3)
        mid[4, elems] = phi.reshape(8, 16, LEV)
        return carry

    lax.fori_loop(0, 4, newton_rows, 0)

    def place_column(j, carry):
        phi = mid[4, cells[0, j]]
        out[5, j] = phi
        out[4, j] = (phi - xc[0, cells[0, j]]) / gravity_step
        return carry

    lax.fori_loop(0, TX * TY, place_column, 0)

    for copy in second_copies:
        copy.wait()
    add_rim(s3, recv3)

    def final_strip(ey, carry):
        here = pl.ds(pl.multiple_of(48 * ey, 16), STRIP)
        inverse = rinv[here] * visc_coef
        nodal = scaled_strip(s3, here, inverse, 4)
        final = strip_of(mid, ey, range(4)) - mm(spread2, stack2(nodal))
        for k in range(4):
            mid[k, pl.ds(TX * ey, TX)] = final[:, k * LEV : (k + 1) * LEV].reshape(TX, 16, LEV)
        return carry

    lax.fori_loop(0, TY, final_strip, 0)

    def place_fields(j, carry):
        for k in range(4):
            out[k, j] = mid[k, cells[0, j]]
        return carry

    lax.fori_loop(0, TX * TY, place_fields, 0)


def store_kernel(fields, *refs):
    outs, sem = refs[:FIELDS], refs[FIELDS]
    copies = [pltpu.make_async_copy(fields.at[k], outs[k], sem.at[k]) for k in range(FIELDS)]
    for copy in copies:
        copy.start()
    for copy in copies:
        copy.wait()


def per_device(pot_temp, tracer, wind_u, wind_v, vert_w, geopot, elem_mass, deriv_x, deriv_y, col_inverse, element_cell):
    shape = pot_temp.shape
    vmem = pl.BlockSpec(memory_space=pltpu.VMEM)
    smem = pl.BlockSpec(memory_space=pltpu.SMEM)
    hbm = pl.BlockSpec(memory_space=pl.ANY)
    rim = sum(COUNT)
    fields = pl.pallas_call(
        step_kernel,
        out_shape=pltpu.VMEM((FIELDS,) + shape, F32),
        in_specs=[hbm] * 6 + [vmem] * 4 + [smem, vmem],
        out_specs=vmem,
        scratch_shapes=[
            pltpu.VMEM((FIELDS,) + shape, F32),
            pltpu.VMEM((FIELDS,) + shape, F32),
            pltpu.VMEM((5,) + shape, F32),
            pltpu.VMEM((5, NODES, LEV), F32),
            pltpu.VMEM((4, NODES, LEV), F32),
            pltpu.VMEM((4, NODES, LEV), F32),
            pltpu.VMEM((1, NODES, LEV), F32),
            pltpu.VMEM((NODES, LEV), F32),
            pltpu.VMEM((512, LEV), F32),
            pltpu.VMEM((2, TY, STRIP, 3 * STRIP), BF16),
            pltpu.SMEM((TX * TY,), jnp.int32),
            pltpu.VMEM((1, rim, LEV), F32),
            pltpu.VMEM((1, rim, LEV), F32),
            pltpu.VMEM((5, rim, LEV), F32),
            pltpu.VMEM((5, rim, LEV), F32),
            pltpu.VMEM((4, rim, LEV), F32),
            pltpu.VMEM((4, rim, LEV), F32),
            pltpu.VMEM((4, rim, LEV), F32),
            pltpu.VMEM((4, rim, LEV), F32),
            pltpu.SemaphoreType.DMA((6,)),
            pltpu.SemaphoreType.DMA((4, 8)),
            pltpu.SemaphoreType.DMA((4, 8)),
        ],
        compiler_params=pltpu.CompilerParams(collective_id=0, has_side_effects=True, vmem_limit_bytes=62 << 20),
    )(pot_temp, tracer, wind_u, wind_v, vert_w, geopot, elem_mass.T, deriv_x, deriv_y, col_inverse, element_cell, element_cell)
    result = jax.ShapeDtypeStruct(shape, F32)
    return tuple(
        pl.pallas_call(
            store_kernel,
            out_shape=[result] * FIELDS,
            in_specs=[vmem],
            out_specs=[hbm] * FIELDS,
            scratch_shapes=[pltpu.SemaphoreType.DMA((FIELDS,))],
            compiler_params=pltpu.CompilerParams(vmem_limit_bytes=48 << 20),
        )(fields)
    )


def solution(mesh):
    field = P(("sfc", "sub"), None, None)
    flat = P(("sfc", "sub"), None)
    return jax.shard_map(
        per_device,
        mesh=mesh,
        in_specs=(field,) * 6 + (flat, P(), P(), P(), flat),
        out_specs=(field,) * 6,
        check_vma=False,
    )
```

```python
import jax
import jax.numpy as jnp
from jax import lax
from jax.experimental import pallas as pl
from jax.experimental.pallas import tpu as pltpu
from jax.sharding import PartitionSpec as P

TX = 4
TY = 8
LEV = 128
NEWTON = 3
PITCH = 16
ROWS = 3 * TY + 1
NODES = ROWS * PITCH
STRIP = 64
FIELDS = 6

time_step = 0.4
visc_coef = 0.1
buoyancy = 0.5
gravity_step = 0.5
column_couple = 0.25

F32 = jnp.float32
BF16 = jnp.bfloat16
MESH = pl.DeviceIdType.MESH

SIDES = ((0, -1), (0, 1), (-1, 0), (1, 0), (-1, -1), (-1, 1), (1, -1), (1, 1))
OPPOSITE = (1, 0, 3, 2, 7, 6, 5, 4)
OFFSET = (0, 32, 64, 80, 96, 104, 112, 120)
COUNT = (32, 32, 16, 16, 8, 8, 8, 8)
CORNER_NODE = (0, 12, NODES - PITCH, NODES - PITCH + 12)


def iota(shape, dim):
    return lax.broadcasted_iota(jnp.int32, shape, dim)


def halves(x):
    high = x.astype(BF16)
    return high, (x - high.astype(F32)).astype(BF16)


def stack2(x):
    high, low = halves(x)
    return jnp.concatenate([high, low], axis=0)


def stack3(x):
    high, low = halves(x)
    return jnp.concatenate([high, low, high], axis=0)


def weight3(x):
    high, low = halves(x)
    return jnp.where(iota(x.shape, 1) < 2 * (x.shape[1] // 3), high.astype(F32), low.astype(F32)).astype(BF16)


def mm(a, b):
    return jnp.dot(a, b, preferred_element_type=F32)


def exact(a, b):
    return jnp.dot(a, b, preferred_element_type=F32, precision=lax.Precision.HIGHEST)


def onehot(cond):
    return jnp.where(cond, 1.0, 0.0).astype(F32)


def block_diag(matrix, cols):
    left = onehot(iota((STRIP, 16), 0) % 16 == iota((STRIP, 16), 1))
    right = onehot(iota((16, cols), 1) % 16 == iota((16, cols), 0))
    spread = exact(exact(left, matrix), right)
    same = (iota((STRIP, cols), 1) % STRIP) // 16 == iota((STRIP, cols), 0) // 16
    return jnp.where(same, spread, 0.0)


def node_point(node, point):
    return (node // PITCH == (point % 16) // 4) & (node % PITCH == 3 * (point // 16) + point % 4)


def gather_rim(grid, send):
    for k in range(grid.shape[0]):
        send[k, 0:ROWS] = grid[k, pl.ds(0, ROWS, stride=PITCH)]
        send[k, 32 : 32 + ROWS] = grid[k, pl.ds(12, ROWS, stride=PITCH)]
        send[k, 64:80] = grid[k, 0:16]
        send[k, 80:96] = grid[k, NODES - 16 : NODES]
        for corner, node in enumerate(CORNER_NODE):
            send[k, 96 + 8 * corner : 97 + 8 * corner] = grid[k, node : node + 1]


def add_rim(grid, recv):
    for k in range(grid.shape[0]):
        for first, rows in ((0, pl.ds(0, ROWS, stride=PITCH)), (32, pl.ds(12, ROWS, stride=PITCH))):
            grid[k, rows] = grid[k, rows] + recv[k, first : first + ROWS]
        grid[k, 0:16] = grid[k, 0:16] + recv[k, 64:80]
        grid[k, NODES - 16 : NODES] = grid[k, NODES - 16 : NODES] + recv[k, 80:96]
        for corner, node in enumerate(CORNER_NODE):
            grid[k, node : node + 1] = grid[k, node : node + 1] + recv[k, 96 + 8 * corner : 97 + 8 * corner]


def step_kernel(
    pot_in, tracer_in, u_in, v_in, w_in, geo_in, mass_in, dx_in, dy_in, col_in, cells, cells_row,
    out,
    xin, xc, mid, s1, s2, s3, mgrid, rinv, mcol, kmat, inv,
    send0, recv0, send1, recv1, send2, recv2, send3, recv3,
    load_sem, send_sem, recv_sem,
):
    row = lax.axis_index("sfc")
    col = lax.axis_index("sub")
    n_row = lax.axis_size("sfc")
    n_col = lax.axis_size("sub")

    def device(side):
        return (lax.rem(row + side[0] + n_row, n_row), lax.rem(col + side[1] + n_col, n_col))

    barrier = pltpu.get_barrier_semaphore()
    for side in SIDES:
        pl.semaphore_signal(barrier, inc=1, device_id=device(side), device_id_type=MESH)

    sources = (geo_in, w_in, pot_in, tracer_in, u_in, v_in)
    loads = [pltpu.make_async_copy(ref, xin.at[k], load_sem.at[k]) for k, ref in enumerate(sources)]
    for load in loads:
        load.start()

    def exchange(turn, send, recv):
        copies = []
        for k in range(8):
            copies.append(
                pltpu.make_async_remote_copy(
                    src_ref=send.at[:, pl.ds(OFFSET[k], COUNT[k])],
                    dst_ref=recv.at[:, pl.ds(OFFSET[OPPOSITE[k]], COUNT[k])],
                    send_sem=send_sem.at[turn, k],
                    recv_sem=recv_sem.at[turn, OPPOSITE[k]],
                    device_id=device(SIDES[k]),
                    device_id_type=MESH,
                )
            )
        return copies

    def invert(c, carry):
        slot = jnp.int32(0)
        for j in range(TX * TY):
            slot = jnp.where(cells[0, j] == c, j, slot)
        inv[c] = slot
        return carry

    lax.fori_loop(0, TX * TY, invert, 0)

    dx = dx_in[...]
    dy = dy_in[...]
    lap = exact(dx, dx) + exact(dy, dy)
    lap_blk = block_diag(lap, 3 * STRIP)
    deriv3 = weight3(jnp.concatenate([block_diag(dx, 3 * STRIP), block_diag(dy, 3 * STRIP)], axis=0))
    spread3 = onehot(node_point(iota((STRIP, 3 * STRIP), 1) % STRIP, iota((STRIP, 3 * STRIP), 0)))
    lap_nodes = exact(block_diag(lap, STRIP), spread3)
    gather2 = onehot(node_point(iota((STRIP, 2 * STRIP), 0), iota((STRIP, 2 * STRIP), 1) % STRIP)).astype(BF16)
    spread2 = onehot(node_point(iota((STRIP, 2 * STRIP), 1) % STRIP, iota((STRIP, 2 * STRIP), 0))).astype(BF16)

    for send in (send0, send1, send2, send3):
        send[...] = jnp.zeros_like(send)
    for grid in (s1, s2, s3, mgrid):
        grid[:, 0:16] = jnp.zeros((grid.shape[0], 16, LEV), F32)

    def accumulate(grid, start, vals):
        head = pl.ds(start, 16)
        tail = pl.ds(pl.multiple_of(start + 16, 16), STRIP - 16)
        for k in range(grid.shape[0]):
            part = vals[:, k * LEV : (k + 1) * LEV]
            grid[k, head] = grid[k, head] + part[0:16]
            grid[k, tail] = part[16:]

    def scaled_strip(grid, here, inverse, count):
        return jnp.concatenate([grid[k, here] * inverse for k in range(count)], axis=1)

    def mass_strip(ey, carry):
        points = []
        for ex in range(TX):
            chosen = jnp.where(cells_row[...] == TX * ey + ex, mass_in[...], 0.0)
            points.append(jnp.broadcast_to(jnp.sum(chosen, axis=1, keepdims=True), (16, LEV)))
        strip_mass = jnp.concatenate(points, axis=0)
        mcol[pl.ds(pl.multiple_of(STRIP * ey, STRIP), STRIP)] = strip_mass
        accumulate(mgrid, pl.multiple_of(48 * ey, 16), mm(gather2, stack2(strip_mass)))
        wide = jnp.concatenate([strip_mass, strip_mass[:, :STRIP]], axis=1)
        kmat[0, ey] = weight3(mm(gather2, stack2(wide * lap_blk)))
        kmat[1, ey] = weight3(mm(gather2, stack2(wide * lap_nodes)))
        return carry

    lax.fori_loop(0, TY, mass_strip, 0, unroll=True)
    gather_rim(mgrid, send0)
    pl.semaphore_wait(barrier, 8)
    mass_copies = exchange(0, send0, recv0)
    for copy in mass_copies:
        copy.start()

    for load in loads:
        load.wait()

    def strip_of(ref, ey, fields):
        return jnp.concatenate([ref[k, pl.ds(TX * ey, TX)].reshape(STRIP, LEV) for k in fields], axis=1)

    def tend_strip(ey, carry):
        points = pl.ds(pl.multiple_of(STRIP * ey, STRIP), STRIP)
        for ex in range(TX):
            slot = inv[TX * ey + ex]
            for k in range(FIELDS):
                xc[k, TX * ey + ex] = xin[k, slot]
        x = strip_of(xc, ey, range(FIELDS))
        x3 = stack3(x)
        slopes = mm(deriv3, x3[:, : 4 * LEV])
        sx = slopes[:STRIP]
        sy = slopes[STRIP:]
        pot = x[:, 2 * LEV : 3 * LEV]
        u = x[:, 4 * LEV : 5 * LEV]
        v = x[:, 5 * LEV : 6 * LEV]

        def advect(k):
            cols = slice(k * LEV, (k + 1) * LEV)
            return -(u * sx[:, cols] + v * sy[:, cols])

        tend = [advect(2), advect(3), -sx[:, :LEV], -sy[:, :LEV], advect(1) + buoyancy * pot]
        weight = mcol[points]
        weighted = jnp.concatenate([t * weight for t in tend], axis=1)
        start = pl.multiple_of(48 * ey, 16)
        accumulate(s1, start, mm(gather2, stack2(weighted)))
        accumulate(s2, start, mm(kmat[0, ey], x3[:, 2 * LEV :]))
        return carry

    lax.fori_loop(0, TY, tend_strip, 0, unroll=True)
    gather_rim(s1, send1)
    tend_copies = exchange(1, send1, recv1)
    for copy in tend_copies:
        copy.start()

    for copy in mass_copies:
        copy.wait()
    add_rim(mgrid, recv0)
    total_mass = mgrid[0]
    rinv[...] = jnp.where(total_mass > 0.0, 1.0 / jnp.where(total_mass > 0.0, total_mass, 1.0), 0.0)

    for copy in tend_copies:
        copy.wait()
    add_rim(s1, recv1)

    def lap_strip(source, scale):
        def body(ey, carry):
            start = pl.multiple_of(48 * ey, 16)
            here = pl.ds(start, STRIP)
            inverse = rinv[here] * scale
            nodal = scaled_strip(source, here, inverse, 4)
            vals = mm(kmat[1, ey], stack3(nodal))
            if source is s1:
                for k in range(4):
                    s2[k, here] = s2[k, here] + vals[:, k * LEV : (k + 1) * LEV]
            else:
                accumulate(s3, start, vals)
            return carry

        return body

    lax.fori_loop(0, TY, lap_strip(s1, time_step), 0, unroll=True)
    gather_rim(s2, send2)
    first_copies = exchange(2, send2, recv2)
    for copy in first_copies:
        copy.start()

    def mid_strip(ey, carry):
        here = pl.ds(pl.multiple_of(48 * ey, 16), STRIP)
        inverse = rinv[here] * time_step
        nodal = scaled_strip(s1, here, inverse, 5)
        change = mm(spread2, stack2(nodal))
        state = strip_of(xc, ey, (2, 3, 4, 5, 1)) + change
        for k in range(5):
            mid[k, pl.ds(TX * ey, TX)] = state[:, k * LEV : (k + 1) * LEV].reshape(TX, 16, LEV)
        return carry

    lax.fori_loop(0, TY, mid_strip, 0, unroll=True)

    for copy in first_copies:
        copy.wait()
    add_rim(s2, recv2)
    lax.fori_loop(0, TY, lap_strip(s2, 1.0), 0, unroll=True)
    gather_rim(s3, send3)
    second_copies = exchange(3, send3, recv3)
    for copy in second_copies:
        copy.start()

    col_high, col_low = halves(col_in[...])
    col3 = jnp.concatenate([col_high, col_high, col_low], axis=0)
    lane = iota((128, LEV), 1)

    def newton_rows(part, carry):
        elems = pl.ds(8 * part, 8)
        geo = xc[0, elems].reshape(128, LEV)
        target = geo + gravity_step * mid[4, elems].reshape(128, LEV)
        phi = target
        for _ in range(NEWTON):
            above = jnp.where(lane == LEV - 1, 0.0, pltpu.roll(phi, LEV - 1, 1))
            flux = jnp.tanh(above - phi)
            below = jnp.where(lane == 0, 0.0, pltpu.roll(flux, 1, 1))
            resid = phi - target - column_couple * (flux - below)
            high, low = halves(resid)
            phi = phi - mm(jnp.concatenate([high, low, high], axis=1), col3)
        mid[4, elems] = phi.reshape(8, 16, LEV)
        return carry

    lax.fori_loop(0, 4, newton_rows, 0, unroll=True)

    def place_column(j, carry):
        phi = mid[4, cells[0, j]]
        out[5, j] = phi
        out[4, j] = (phi - xc[0, cells[0, j]]) / gravity_step
        return carry

    lax.fori_loop(0, TX * TY, place_column, 0, unroll=True)

    for copy in second_copies:
        copy.wait()
    add_rim(s3, recv3)

    def final_strip(ey, carry):
        here = pl.ds(pl.multiple_of(48 * ey, 16), STRIP)
        inverse = rinv[here] * visc_coef
        nodal = scaled_strip(s3, here, inverse, 4)
        final = strip_of(mid, ey, range(4)) - mm(spread2, stack2(nodal))
        for k in range(4):
            mid[k, pl.ds(TX * ey, TX)] = final[:, k * LEV : (k + 1) * LEV].reshape(TX, 16, LEV)
        return carry

    lax.fori_loop(0, TY, final_strip, 0, unroll=True)

    def place_fields(j, carry):
        for k in range(4):
            out[k, j] = mid[k, cells[0, j]]
        return carry

    lax.fori_loop(0, TX * TY, place_fields, 0, unroll=True)


def store_kernel(fields, *refs):
    outs, sem = refs[:FIELDS], refs[FIELDS]
    copies = [pltpu.make_async_copy(fields.at[k], outs[k], sem.at[k]) for k in range(FIELDS)]
    for copy in copies:
        copy.start()
    for copy in copies:
        copy.wait()


def per_device(pot_temp, tracer, wind_u, wind_v, vert_w, geopot, elem_mass, deriv_x, deriv_y, col_inverse, element_cell):
    shape = pot_temp.shape
    vmem = pl.BlockSpec(memory_space=pltpu.VMEM)
    smem = pl.BlockSpec(memory_space=pltpu.SMEM)
    hbm = pl.BlockSpec(memory_space=pl.ANY)
    rim = sum(COUNT)
    fields = pl.pallas_call(
        step_kernel,
        out_shape=pltpu.VMEM((FIELDS,) + shape, F32),
        in_specs=[hbm] * 6 + [vmem] * 4 + [smem, vmem],
        out_specs=vmem,
        scratch_shapes=[
            pltpu.VMEM((FIELDS,) + shape, F32),
            pltpu.VMEM((FIELDS,) + shape, F32),
            pltpu.VMEM((5,) + shape, F32),
            pltpu.VMEM((5, NODES, LEV), F32),
            pltpu.VMEM((4, NODES, LEV), F32),
            pltpu.VMEM((4, NODES, LEV), F32),
            pltpu.VMEM((1, NODES, LEV), F32),
            pltpu.VMEM((NODES, LEV), F32),
            pltpu.VMEM((512, LEV), F32),
            pltpu.VMEM((2, TY, STRIP, 3 * STRIP), BF16),
            pltpu.SMEM((TX * TY,), jnp.int32),
            pltpu.VMEM((1, rim, LEV), F32),
            pltpu.VMEM((1, rim, LEV), F32),
            pltpu.VMEM((5, rim, LEV), F32),
            pltpu.VMEM((5, rim, LEV), F32),
            pltpu.VMEM((4, rim, LEV), F32),
            pltpu.VMEM((4, rim, LEV), F32),
            pltpu.VMEM((4, rim, LEV), F32),
            pltpu.VMEM((4, rim, LEV), F32),
            pltpu.SemaphoreType.DMA((6,)),
            pltpu.SemaphoreType.DMA((4, 8)),
            pltpu.SemaphoreType.DMA((4, 8)),
        ],
        compiler_params=pltpu.CompilerParams(collective_id=0, has_side_effects=True, vmem_limit_bytes=62 << 20),
    )(pot_temp, tracer, wind_u, wind_v, vert_w, geopot, elem_mass.T, deriv_x, deriv_y, col_inverse, element_cell, element_cell)
    result = jax.ShapeDtypeStruct(shape, F32)
    return tuple(
        pl.pallas_call(
            store_kernel,
            out_shape=[result] * FIELDS,
            in_specs=[vmem],
            out_specs=[hbm] * FIELDS,
            scratch_shapes=[pltpu.SemaphoreType.DMA((FIELDS,))],
            compiler_params=pltpu.CompilerParams(vmem_limit_bytes=48 << 20),
        )(fields)
    )


def solution(mesh):
    field = P(("sfc", "sub"), None, None)
    flat = P(("sfc", "sub"), None)
    return jax.shard_map(
        per_device,
        mesh=mesh,
        in_specs=(field,) * 6 + (flat, P(), P(), P(), flat),
        out_specs=(field,) * 6,
        check_vma=False,
    )
```

```python
import jax
import jax.numpy as jnp
import numpy as np
from jax import lax
from jax.experimental import pallas as pl
from jax.experimental.pallas import tpu as pltpu
from jax.sharding import PartitionSpec as P

TX = 4
TY = 8
LEV = 128
NEWTON = 3
PITCH = 16
ROWS = 3 * TY + 1
NODES = ROWS * PITCH
STRIP = 64
FIELDS = 6

time_step = 0.4
visc_coef = 0.1
buoyancy = 0.5
gravity_step = 0.5
column_couple = 0.25

F32 = jnp.float32
BF16 = jnp.bfloat16
MESH = pl.DeviceIdType.MESH

SIDES = ((0, -1), (0, 1), (-1, 0), (1, 0), (-1, -1), (-1, 1), (1, -1), (1, 1))
OPPOSITE = (1, 0, 3, 2, 7, 6, 5, 4)
OFFSET = (0, 32, 64, 88, 112, 120, 128, 136)
COUNT = (32, 32, 24, 24, 8, 8, 8, 8)
RIM = 144
LINE_COUNT = (25, 25, 13, 13, 1, 1, 1, 1)
LINES = (
    (0, 25, 0, 16), (32, 25, 12, 16), (64, 13, 0, 1), (88, 13, 384, 1),
    (112, 1, 0, 1), (120, 1, 12, 1), (128, 1, 384, 1), (136, 1, 396, 1),
)
ARMS = (
    (25, 3, 1, 1), (28, 3, 385, 1), (57, 3, 9, 1), (60, 3, 393, 1),
    (77, 3, 16, 16), (80, 3, 28, 16), (101, 3, 336, 16), (104, 3, 348, 16),
    (113, 3, 1, 1), (116, 3, 16, 16), (121, 3, 9, 1), (124, 3, 28, 16),
    (129, 3, 385, 1), (132, 3, 336, 16), (137, 3, 393, 1), (140, 3, 348, 16),
)


def rim_tables():
    node = np.full(RIM, -1)
    line = np.zeros(RIM)
    for group in (LINES, ARMS):
        for first, rows, start, stride in group:
            node[first : first + rows] = start + stride * np.arange(rows)
            line[first : first + rows] = group is LINES
    place = np.arange(RIM) - 4000.0
    slot = np.zeros(RIM)
    lane_node = np.full(RIM, -1)
    for k in range(8):
        mine = np.arange(OFFSET[k], OFFSET[k] + COUNT[k])
        theirs = mine - OFFSET[k] + OFFSET[OPPOSITE[k]]
        slot[mine] = k
        lane_node[mine] = node[theirs]
        known = node[theirs] >= 0
        ny = node[theirs] // PITCH + 3 * TY * SIDES[k][0]
        nx = node[theirs] % PITCH + 3 * TX * SIDES[k][1]
        place[mine[known]] = ((ny + 8) * 64 + nx + 8)[known]
    unique = line.copy()
    unique[112:] = 0
    unique[[64, 76, 88, 100]] = 0
    rows = np.stack([np.broadcast_to(t[:, None], (RIM, LEV)) for t in (place, line, unique, slot)])
    lanes = np.full((3, 8, 2 * LEV), -9000.0)
    lanes[:, :, :RIM] = np.stack([lane_node, place, slot])[:, None]
    return rows.astype(np.float32), lanes.astype(np.float32)


def iota(shape, dim):
    return lax.broadcasted_iota(jnp.int32, shape, dim)


def halves(x):
    high = x.astype(BF16)
    return high, (x - high.astype(F32)).astype(BF16)


def stack2(x):
    high, low = halves(x)
    return jnp.concatenate([high, low], axis=0)


def stack3(x):
    high, low = halves(x)
    return jnp.concatenate([high, low, high], axis=0)


def weight3(x):
    high, low = halves(x)
    return jnp.where(iota(x.shape, 1) < 2 * (x.shape[1] // 3), high.astype(F32), low.astype(F32)).astype(BF16)


def mm(a, b):
    return jnp.dot(a, b, preferred_element_type=F32)


def exact(a, b):
    return jnp.dot(a, b, preferred_element_type=F32, precision=lax.Precision.HIGHEST)


def onehot(cond):
    return jnp.where(cond, 1.0, 0.0).astype(F32)


def block_diag(matrix, cols):
    left = onehot(iota((STRIP, 16), 0) % 16 == iota((STRIP, 16), 1))
    right = onehot(iota((16, cols), 1) % 16 == iota((16, cols), 0))
    spread = exact(exact(left, matrix), right)
    same = (iota((STRIP, cols), 1) % STRIP) // 16 == iota((STRIP, cols), 0) // 16
    return jnp.where(same, spread, 0.0)


def node_point(node, point):
    return (node // PITCH == (point % 16) // 4) & (node % PITCH == 3 * (point // 16) + point % 4)


def gather_rim(grid, send, groups, blocks, first=0):
    for n, k in enumerate(blocks):
        for group in groups:
            for row, rows, start, stride in group:
                send[first + n, row : row + rows] = grid[k, pl.ds(start, rows, stride=stride)]


def add_rim(grid, recv, blocks):
    for k in blocks:
        for row, rows, start, stride in LINES:
            nodes = pl.ds(start, rows, stride=stride)
            grid[k, nodes] = grid[k, nodes] + recv[k, row : row + rows]


def lanes_of(ref, blocks):
    return jnp.concatenate([ref[k] for k in blocks], axis=1)


def swap_sides(x):
    return jnp.concatenate([x[OFFSET[k] : OFFSET[k] + COUNT[k]] for k in OPPOSITE], axis=0)


def mm3(weight, x):
    w_high, w_low = halves(weight[:, :RIM])
    high, low = halves(x)
    return mm(w_high, high) + mm(w_high, low) + mm(w_low, high)


def step_kernel(
    pot_in, tracer_in, u_in, v_in, w_in, geo_in, mass_hbm, dx_hbm, dy_hbm, col_hbm, cells_hbm, row_hbm, lane_hbm,
    out,
    mass_in, dx_in, dy_in, col_in, cells, cells_row, row_tab, lane_tab,
    xin, xc, mid, s1, s2, s3, s4, mgrid, rinv, mcol, kmat, inv,
    send0, recv0, send1, recv1, send2, recv2, send3, recv3, local, foreign, rim_inv,
    load_sem, send_sem, recv_sem,
):
    row = lax.axis_index("sfc")
    col = lax.axis_index("sub")
    n_row = lax.axis_size("sfc")
    n_col = lax.axis_size("sub")

    def device(side):
        return (lax.rem(row + side[0] + n_row, n_row), lax.rem(col + side[1] + n_col, n_col))

    barrier = pltpu.get_barrier_semaphore()
    for side in SIDES:
        pl.semaphore_signal(barrier, inc=1, device_id=device(side), device_id_type=MESH)

    sources = (geo_in, w_in, pot_in, tracer_in, u_in, v_in)
    loads = [pltpu.make_async_copy(ref, xin.at[k], load_sem.at[k]) for k, ref in enumerate(sources)]
    smalls = [
        pltpu.make_async_copy(source, place, load_sem.at[FIELDS + k])
        for k, (source, place) in enumerate(
            (
                (cells_hbm, cells), (cells_hbm, cells_row), (mass_hbm, mass_in), (dx_hbm, dx_in), (dy_hbm, dy_in),
                (col_hbm, col_in), (row_hbm, row_tab), (lane_hbm, lane_tab),
            )
        )
    ]
    for load in smalls + loads:
        load.start()

    def exchange(turn, send, recv, counts, offset=OFFSET):
        copies = []
        for k in (2, 3, 4, 5, 6, 7, 0, 1):
            copies.append(
                pltpu.make_async_remote_copy(
                    src_ref=send.at[:, pl.ds(offset[k], counts[k])],
                    dst_ref=recv.at[:, pl.ds(offset[OPPOSITE[k]], counts[k])],
                    send_sem=send_sem.at[turn, k],
                    recv_sem=recv_sem.at[turn, OPPOSITE[k]],
                    device_id=device(SIDES[k]),
                    device_id_type=MESH,
                )
            )
        return copies

    for load in smalls:
        load.wait()

    def invert(c, carry):
        slot = jnp.int32(0)
        for j in range(TX * TY):
            slot = jnp.where(cells[0, j] == c, j, slot)
        inv[c] = slot
        return carry

    lax.fori_loop(0, TX * TY, invert, 0)

    dx = dx_in[...]
    dy = dy_in[...]
    deriv3 = weight3(jnp.concatenate([block_diag(dx, 3 * STRIP), block_diag(dy, 3 * STRIP)], axis=0))
    gather2 = onehot(node_point(iota((STRIP, 2 * STRIP), 0), iota((STRIP, 2 * STRIP), 1) % STRIP)).astype(BF16)
    spread2 = onehot(node_point(iota((STRIP, 2 * STRIP), 1) % STRIP, iota((STRIP, 2 * STRIP), 0))).astype(BF16)

    for send in (send0, send1, local):
        send[...] = jnp.zeros_like(send)
    for grid in (s1, s2, s3, s4, mgrid):
        grid[:, 0:16] = jnp.zeros((grid.shape[0], 16, LEV), F32)

    def accumulate(grid, start, vals):
        head = pl.ds(start, 16)
        tail = pl.ds(pl.multiple_of(start + 16, 16), STRIP - 16)
        for k in range(grid.shape[0]):
            part = vals[:, k * LEV : (k + 1) * LEV]
            grid[k, head] = grid[k, head] + part[0:16]
            grid[k, tail] = part[16:]

    def scaled_strip(grid, here, inverse, count):
        return jnp.concatenate([grid[k, here] * inverse for k in range(count)], axis=1)

    def mass_strip(ey, carry):
        points = []
        for ex in range(TX):
            chosen = jnp.where(cells_row[...] == TX * ey + ex, mass_in[...], 0.0)
            points.append(jnp.broadcast_to(jnp.sum(chosen, axis=1, keepdims=True), (16, LEV)))
        strip_mass = jnp.concatenate(points, axis=0)
        mcol[pl.ds(pl.multiple_of(STRIP * ey, STRIP), STRIP)] = strip_mass
        accumulate(mgrid, pl.multiple_of(48 * ey, 16), mm(gather2, stack2(strip_mass)))
        return carry

    lax.fori_loop(0, TY, mass_strip, 0, unroll=True)
    gather_rim(mgrid, send0, (LINES, ARMS), range(1))
    for load in loads:
        load.wait()

    def strip_of(ref, ey, fields):
        return jnp.concatenate([ref[k, pl.ds(TX * ey, TX)].reshape(STRIP, LEV) for k in fields], axis=1)

    def tend_strip(ey, carry):
        points = pl.ds(pl.multiple_of(STRIP * ey, STRIP), STRIP)
        for ex in range(TX):
            slot = inv[TX * ey + ex]
            for k in range(FIELDS):
                xc[k, TX * ey + ex] = xin[k, slot]
        x = strip_of(xc, ey, range(FIELDS))
        slopes = mm(deriv3, stack3(x[:, : 4 * LEV]))
        sx = slopes[:STRIP]
        sy = slopes[STRIP:]
        pot = x[:, 2 * LEV : 3 * LEV]
        u = x[:, 4 * LEV : 5 * LEV]
        v = x[:, 5 * LEV : 6 * LEV]

        def advect(k):
            cols = slice(k * LEV, (k + 1) * LEV)
            return -(u * sx[:, cols] + v * sy[:, cols])

        tend = [advect(2), advect(3), -sx[:, :LEV], -sy[:, :LEV], advect(1) + buoyancy * pot]
        weight = mcol[points]
        weighted = jnp.concatenate([t * weight for t in tend], axis=1)
        start = pl.multiple_of(48 * ey, 16)
        accumulate(s1, start, mm(gather2, stack2(weighted)))
        return carry

    lax.fori_loop(0, TY, tend_strip, 0, unroll=True)
    gather_rim(s1, send1, (LINES,), range(5))
    pl.semaphore_wait(barrier, 8)
    mass_copies = exchange(0, send0, recv0, COUNT)
    tend_copies = exchange(1, send1.at[pl.ds(0, 4)], recv1.at[pl.ds(0, 4)], LINE_COUNT)
    for copy in mass_copies + tend_copies:
        copy.start()

    lap = exact(dx, dx) + exact(dy, dy)
    lap_blk = block_diag(lap, 3 * STRIP)
    spread3 = onehot(node_point(iota((STRIP, 3 * STRIP), 1) % STRIP, iota((STRIP, 3 * STRIP), 0)))
    lap_nodes = exact(block_diag(lap, STRIP), spread3)

    def matrix_strip(ey, carry):
        strip_mass = mcol[pl.ds(pl.multiple_of(STRIP * ey, STRIP), STRIP)]
        wide = jnp.concatenate([strip_mass, strip_mass[:, :STRIP]], axis=1)
        kmat[0, ey] = weight3(mm(gather2, stack2(wide * lap_blk)))
        kmat[1, ey] = weight3(mm(gather2, stack2(wide * lap_nodes)))
        return carry

    lax.fori_loop(0, TY, matrix_strip, 0, unroll=True)

    same_place = onehot(row_tab[0][:, :1] == lane_tab[1][0:1, :RIM]).astype(BF16)

    def merge(x):
        high, low = halves(x)
        return mm(same_place, high) + mm(same_place, low)

    def reciprocal(total):
        return jnp.where(total > 0.0, 1.0 / jnp.where(total > 0.0, total, 1.0), 0.0)

    line = row_tab[1]
    unique = row_tab[2]
    node_row = iota((NODES, LEV), 0) // PITCH
    node_col = iota((NODES, LEV), 0) % PITCH
    inside = (node_row > 0) & (node_row < ROWS - 1) & (node_col > 0) & (node_col < 12)
    rinv[1] = jnp.where(inside, reciprocal(mgrid[0]), 0.0)

    def first_strip(ey, carry):
        start = pl.multiple_of(48 * ey, 16)
        here = pl.ds(start, STRIP)
        rims = onehot((iota((STRIP, 2 * LEV), 0) + start).astype(F32) == lane_tab[0][0:1])
        nodal = jnp.concatenate([scaled_strip(s1, here, rinv[1, here] * time_step, 4), rims], axis=1)
        response = mm(kmat[1, ey], stack3(nodal))
        own = mm(kmat[0, ey], stack3(strip_of(xc, ey, (2, 3, 4, 5))))
        accumulate(s2, start, jnp.concatenate([response[:, : 4 * LEV] + own, response[:, 4 * LEV :]], axis=1))
        return carry

    lax.fori_loop(0, TY, first_strip, 0, unroll=True)
    gather_rim(s2, local, (LINES, ARMS), range(6))
    send2[...] = local[4:6]
    matrix_copies = exchange(2, send2, recv2, LINE_COUNT)
    vert_copies = exchange(4, send1.at[pl.ds(4, 1)], recv1.at[pl.ds(4, 1)], LINE_COUNT)
    for copy in matrix_copies + vert_copies:
        copy.start()

    def second_strip(ey, carry):
        start = pl.multiple_of(48 * ey, 16)
        here = pl.ds(start, STRIP)
        accumulate(s3, start, mm(kmat[1, ey], stack3(scaled_strip(s2, here, rinv[1, here], 6))))
        return carry

    lax.fori_loop(0, TY, second_strip, 0, unroll=True)
    gather_rim(s3, local, (LINES,), range(6), 6)

    for copy in mass_copies:
        copy.wait()
    rim_inv[...] = reciprocal(merge(recv0[0]) + line * send0[0])
    for copy in tend_copies:
        copy.wait()
    outer = jnp.concatenate(
        [
            (jnp.where(line > 0.0, recv1[k], 0.0) + unique * send1[k]) * (rim_inv[...] * time_step)
            for k in range(4)
        ],
        axis=1,
    )
    outer = swap_sides(outer)
    one = lanes_of(local, range(4)) + mm3(lanes_of(local, range(4, 6)), outer)
    two = lanes_of(local, range(6, 10)) + mm3(lanes_of(local, range(10, 12)), outer)
    for k in range(4):
        for side in range(8):
            mine = slice(OFFSET[side], OFFSET[side] + COUNT[side])
            first = 2 * OFFSET[side]
            send3[k, first : first + COUNT[side]] = one[mine, k * LEV : (k + 1) * LEV]
            send3[k, first + COUNT[side] : first + 2 * COUNT[side]] = two[mine, k * LEV : (k + 1) * LEV]
    visc_copies = exchange(
        3, send3, recv3, [m + n for m, n in zip(COUNT, LINE_COUNT)], [2 * first for first in OFFSET]
    )
    for copy in visc_copies:
        copy.start()

    for k in range(4):
        foreign[k] = one[:, k * LEV : (k + 1) * LEV]
    add_rim(mgrid, recv0, range(1))
    rinv[0] = reciprocal(mgrid[0])
    add_rim(s1, recv1, range(4))
    rim_nodes = lanes_of(s2, range(4, 6))
    own = lanes_of(s2, range(4)) + mm3(rim_nodes, outer)
    for k in range(4):
        s2[k] = own[:, k * LEV : (k + 1) * LEV]

    def third_strip(ey, carry):
        start = pl.multiple_of(48 * ey, 16)
        here = pl.ds(start, STRIP)
        accumulate(s4, start, mm(kmat[1, ey], stack3(scaled_strip(s2, here, rinv[0, here], 4))))
        return carry

    lax.fori_loop(0, TY, third_strip, 0, unroll=True)

    for copy in vert_copies:
        copy.wait()
    add_rim(s1, recv1, range(4, 5))

    def mid_strip(ey, carry):
        here = pl.ds(pl.multiple_of(48 * ey, 16), STRIP)
        nodal = scaled_strip(s1, here, rinv[0, here] * time_step, 5)
        change = mm(spread2, stack2(nodal))
        state = strip_of(xc, ey, (2, 3, 4, 5, 1)) + change
        for k in range(5):
            mid[k, pl.ds(TX * ey, TX)] = state[:, k * LEV : (k + 1) * LEV].reshape(TX, 16, LEV)
        return carry

    lax.fori_loop(0, TY, mid_strip, 0, unroll=True)

    col_high, col_low = halves(col_in[...])
    col3 = jnp.concatenate([col_high, col_high, col_low], axis=0)
    lane = iota((128, LEV), 1)

    def newton_rows(part, carry):
        elems = pl.ds(8 * part, 8)
        geo = xc[0, elems].reshape(128, LEV)
        target = geo + gravity_step * mid[4, elems].reshape(128, LEV)
        phi = target
        for _ in range(NEWTON):
            above = jnp.where(lane == LEV - 1, 0.0, pltpu.roll(phi, LEV - 1, 1))
            flux = jnp.tanh(above - phi)
            below = jnp.where(lane == 0, 0.0, pltpu.roll(flux, 1, 1))
            resid = phi - target - column_couple * (flux - below)
            high, low = halves(resid)
            phi = phi - mm(jnp.concatenate([high, low, high], axis=1), col3)
        mid[4, elems] = phi.reshape(8, 16, LEV)
        return carry

    lax.fori_loop(0, 4, newton_rows, 0, unroll=True)

    def place_column(j, carry):
        phi = mid[4, cells[0, j]]
        out[5, j] = phi
        out[4, j] = (phi - xc[0, cells[0, j]]) / gravity_step
        return carry

    lax.fori_loop(0, TX * TY, place_column, 0, unroll=True)

    for copy in matrix_copies:
        copy.wait()
    own_block = (row_tab[3][:, :1] == lane_tab[2][0:1]) & (line[:, :1] > 0.0)
    rim_matrix = jnp.where(own_block, lanes_of(recv2, range(2)), 0.0)
    inverse = rim_inv[...]
    own_rim = jnp.concatenate([foreign[k] * (line * inverse) for k in range(4)], axis=1)

    def received(part):
        def rows(k, side):
            first = 2 * OFFSET[side] + part * COUNT[side]
            return recv3[k, first : first + COUNT[side]]

        return [jnp.concatenate([rows(k, side) for side in range(8)], axis=0) for k in range(4)]

    for copy in visc_copies:
        copy.wait()
    arrived = merge(jnp.concatenate(received(0), axis=1)) * jnp.concatenate([inverse] * 4, axis=1)
    turned = jnp.concatenate([jnp.where(line > 0.0, rows, 0.0) for rows in received(1)], axis=1)
    outside = mm3(rim_matrix, arrived + own_rim) + turned
    inner = mm3(rim_nodes, swap_sides(arrived * jnp.concatenate([unique] * 4, axis=1)))
    for k in range(4):
        foreign[k] = outside[:, k * LEV : (k + 1) * LEV]
        s4[k] = s4[k] + inner[:, k * LEV : (k + 1) * LEV]
    add_rim(s4, foreign, range(4))

    def final_strip(ey, carry):
        here = pl.ds(pl.multiple_of(48 * ey, 16), STRIP)
        nodal = scaled_strip(s4, here, rinv[0, here] * visc_coef, 4)
        final = strip_of(mid, ey, range(4)) - mm(spread2, stack2(nodal))
        for k in range(4):
            mid[k, pl.ds(TX * ey, TX)] = final[:, k * LEV : (k + 1) * LEV].reshape(TX, 16, LEV)
        return carry

    lax.fori_loop(0, TY, final_strip, 0, unroll=True)

    def place_fields(j, carry):
        for k in range(4):
            out[k, j] = mid[k, cells[0, j]]
        return carry

    lax.fori_loop(0, TX * TY, place_fields, 0, unroll=True)


def store_kernel(fields, *refs):
    outs, sem = refs[:FIELDS], refs[FIELDS]
    copies = [pltpu.make_async_copy(fields.at[k], outs[k], sem.at[k]) for k in range(FIELDS)]
    for copy in copies:
        copy.start()
    for copy in copies:
        copy.wait()


def per_device(pot_temp, tracer, wind_u, wind_v, vert_w, geopot, elem_mass, deriv_x, deriv_y, col_inverse, element_cell):
    shape = pot_temp.shape
    vmem = pl.BlockSpec(memory_space=pltpu.VMEM)
    hbm = pl.BlockSpec(memory_space=pl.ANY)
    rows, lanes = rim_tables()
    fields = pl.pallas_call(
        step_kernel,
        out_shape=pltpu.VMEM((FIELDS,) + shape, F32),
        in_specs=[hbm] * 13,
        out_specs=vmem,
        scratch_shapes=[
            pltpu.VMEM((16, TX * TY), F32),
            pltpu.VMEM((16, 16), F32),
            pltpu.VMEM((16, 16), F32),
            pltpu.VMEM((LEV, LEV), F32),
            pltpu.SMEM((1, TX * TY), jnp.int32),
            pltpu.VMEM((1, TX * TY), jnp.int32),
            pltpu.VMEM(rows.shape, F32),
            pltpu.VMEM(lanes.shape, F32),
            pltpu.VMEM((FIELDS,) + shape, F32),
            pltpu.VMEM((FIELDS,) + shape, F32),
            pltpu.VMEM((5,) + shape, F32),
            pltpu.VMEM((5, NODES, LEV), F32),
            pltpu.VMEM((6, NODES, LEV), F32),
            pltpu.VMEM((6, NODES, LEV), F32),
            pltpu.VMEM((4, NODES, LEV), F32),
            pltpu.VMEM((1, NODES, LEV), F32),
            pltpu.VMEM((2, NODES, LEV), F32),
            pltpu.VMEM((512, LEV), F32),
            pltpu.VMEM((2, TY, STRIP, 3 * STRIP), BF16),
            pltpu.SMEM((TX * TY,), jnp.int32),
        ]
        + [pltpu.VMEM((blocks, RIM, LEV), F32) for blocks in (1, 1, 5, 5, 2, 2)]
        + [pltpu.VMEM((4, 2 * RIM, LEV), F32)] * 2
        + [pltpu.VMEM((blocks, RIM, LEV), F32) for blocks in (12, 4)]
        + [
            pltpu.VMEM((RIM, LEV), F32),
            pltpu.SemaphoreType.DMA((FIELDS + 8,)),
            pltpu.SemaphoreType.DMA((5, 8)),
            pltpu.SemaphoreType.DMA((5, 8)),
        ],
        compiler_params=pltpu.CompilerParams(collective_id=0, has_side_effects=True, vmem_limit_bytes=62 << 20),
    )(pot_temp, tracer, wind_u, wind_v, vert_w, geopot, elem_mass.T, deriv_x, deriv_y, col_inverse, element_cell, rows, lanes)
    result = jax.ShapeDtypeStruct(shape, F32)
    return tuple(
        pl.pallas_call(
            store_kernel,
            out_shape=[result] * FIELDS,
            in_specs=[vmem],
            out_specs=[hbm] * FIELDS,
            scratch_shapes=[pltpu.SemaphoreType.DMA((FIELDS,))],
            compiler_params=pltpu.CompilerParams(vmem_limit_bytes=48 << 20),
        )(fields)
    )


def solution(mesh):
    field = P(("sfc", "sub"), None, None)
    flat = P(("sfc", "sub"), None)
    return jax.shard_map(
        per_device,
        mesh=mesh,
        in_specs=(field,) * 6 + (flat, P(), P(), P(), flat),
        out_specs=(field,) * 6,
        check_vma=False,
    )
```

```python
import jax
import jax.numpy as jnp
import numpy as np
from jax import lax
from jax.experimental import pallas as pl
from jax.experimental.pallas import tpu as pltpu
from jax.sharding import PartitionSpec as P

TX = 4
TY = 8
LEV = 128
NEWTON = 3
PITCH = 16
ROWS = 3 * TY + 1
NODES = ROWS * PITCH
STRIP = 64
FIELDS = 6

time_step = 0.4
visc_coef = 0.1
buoyancy = 0.5
gravity_step = 0.5
column_couple = 0.25

F32 = jnp.float32
BF16 = jnp.bfloat16
MESH = pl.DeviceIdType.MESH

SIDES = ((0, -1), (0, 1), (-1, 0), (1, 0), (-1, -1), (-1, 1), (1, -1), (1, 1))
OPPOSITE = (1, 0, 3, 2, 7, 6, 5, 4)
OFFSET = (0, 40, 80, 112, 144, 160, 176, 192)
COUNT = (40, 40, 32, 32, 16, 16, 16, 16)
RIM = 208
LINE_COUNT = (25, 25, 13, 13, 1, 1, 1, 1)
NEAR_COUNT = (31, 31, 19, 19, 7, 7, 7, 7)
FULL_COUNT = (37, 37, 25, 25, 13, 13, 13, 13)
DIRECT = (2, 3, 0, 1)
DIAGONAL = (4, 5, 6, 7)
TURN_ROWS = (32, 32, 24, 24)
TURN_OFFSET = (0, 32, 64, 88)
TURN_RIM = 112
LINES = (
    (0, 25, 0, 16), (40, 25, 12, 16), (80, 13, 0, 1), (112, 13, 384, 1),
    (144, 1, 0, 1), (160, 1, 12, 1), (176, 1, 384, 1), (192, 1, 396, 1),
)
NEAR = (
    (25, 3, 1, 1), (28, 3, 385, 1), (65, 3, 9, 1), (68, 3, 393, 1),
    (93, 3, 16, 16), (96, 3, 28, 16), (125, 3, 336, 16), (128, 3, 348, 16),
    (145, 3, 1, 1), (148, 3, 16, 16), (161, 3, 9, 1), (164, 3, 28, 16),
    (177, 3, 385, 1), (180, 3, 336, 16), (193, 3, 393, 1), (196, 3, 348, 16),
)
FAR = (
    (31, 3, 4, 1), (34, 3, 388, 1), (71, 3, 6, 1), (74, 3, 390, 1),
    (99, 3, 64, 16), (102, 3, 76, 16), (131, 3, 288, 16), (134, 3, 300, 16),
    (151, 3, 4, 1), (154, 3, 64, 16), (167, 3, 6, 1), (170, 3, 76, 16),
    (183, 3, 388, 1), (186, 3, 288, 16), (199, 3, 390, 1), (202, 3, 300, 16),
)
SIDE_LINES = ((0, 25, 0, 16), (32, 25, 12, 16), (64, 13, 0, 1), (88, 13, 384, 1))
CORNER_LINES = LINES[4:]
PLACE, KNOWN, LINE, UNIQUE, EDGE, LATE, CLOSE, SLOT = range(8)


def rim_tables():
    node = np.full(RIM, -1)
    line = np.zeros(RIM)
    close = np.zeros(RIM)
    for group in (LINES, NEAR, FAR):
        for first, rows, start, stride in group:
            node[first : first + rows] = start + stride * np.arange(rows)
            line[first : first + rows] = group is LINES
            close[first : first + rows] = group is not FAR
    place = np.arange(RIM) - 4000.0
    slot = np.zeros(RIM)
    lane_node = np.full(RIM, -1)
    for k in range(8):
        mine = np.arange(OFFSET[k], OFFSET[k] + COUNT[k])
        theirs = mine - OFFSET[k] + OFFSET[OPPOSITE[k]]
        slot[mine] = k
        lane_node[mine] = node[theirs]
        known = node[theirs] >= 0
        ny = node[theirs] // PITCH + 3 * TY * SIDES[k][0]
        nx = node[theirs] % PITCH + 3 * TX * SIDES[k][1]
        place[mine[known]] = ((ny + 8) * 64 + nx + 8)[known]
    corner = np.zeros(RIM)
    corner[[0, 24, 40, 64, 80, 92, 112, 124]] = 1
    unique = line * (slot < 4) * np.where(slot < 2, 1, 1 - corner)
    edge = line * (slot < 4) * (1 - corner)
    late = np.where(slot < 4, corner, node >= 0)
    rows = np.zeros((RIM, LEV))
    for column, table in enumerate((place, node >= 0, line, unique, edge, late, close, slot)):
        rows[:, column] = table
    lanes = np.full((3, 8, 2 * LEV), -9000.0)
    lanes[:, :, :RIM] = np.stack([lane_node, place, slot])[:, None]
    return rows.astype(np.float32), lanes.astype(np.float32)


def iota(shape, dim):
    return lax.broadcasted_iota(jnp.int32, shape, dim)


def halves(x):
    high = x.astype(BF16)
    return high, (x - high.astype(F32)).astype(BF16)


def stack2(x):
    high, low = halves(x)
    return jnp.concatenate([high, low], axis=0)


def stack3(x):
    high, low = halves(x)
    return jnp.concatenate([high, low, high], axis=0)


def weight3(x):
    high, low = halves(x)
    return jnp.where(iota(x.shape, 1) < 2 * (x.shape[1] // 3), high.astype(F32), low.astype(F32)).astype(BF16)


def mm(a, b):
    return jnp.dot(a, b, preferred_element_type=F32)


def exact(a, b):
    return jnp.dot(a, b, preferred_element_type=F32, precision=lax.Precision.HIGHEST)


def onehot(cond):
    return jnp.where(cond, 1.0, 0.0).astype(F32)


def block_diag(matrix, cols):
    left = onehot(iota((STRIP, 16), 0) % 16 == iota((STRIP, 16), 1))
    right = onehot(iota((16, cols), 1) % 16 == iota((16, cols), 0))
    spread = exact(exact(left, matrix), right)
    same = (iota((STRIP, cols), 1) % STRIP) // 16 == iota((STRIP, cols), 0) // 16
    return jnp.where(same, spread, 0.0)


def node_point(node, point):
    return (node // PITCH == (point % 16) // 4) & (node % PITCH == 3 * (point // 16) + point % 4)


def gather_rim(grid, send, groups, blocks, first=0):
    for n, k in enumerate(blocks):
        for group in groups:
            for row, rows, start, stride in group:
                send[first + n, row : row + rows] = grid[k, pl.ds(start, rows, stride=stride)]


def add_rim(grid, recv, blocks, lines=LINES):
    for k in blocks:
        for row, rows, start, stride in lines:
            nodes = pl.ds(start, rows, stride=stride)
            grid[k, nodes] = grid[k, nodes] + recv[k, row : row + rows]


def lanes_of(ref, blocks):
    return jnp.concatenate([ref[k] for k in blocks], axis=1)


def spread_rows(parts):
    filled = []
    for k, part in enumerate(parts):
        filled.append(part)
        if part.shape[0] < COUNT[k]:
            filled.append(jnp.zeros((COUNT[k] - part.shape[0], part.shape[1]), F32))
    return jnp.concatenate(filled, axis=0)


def swap_sides(x):
    return jnp.concatenate([x[OFFSET[k] : OFFSET[k] + COUNT[k]] for k in OPPOSITE], axis=0)


def mm3(weight, x):
    w_high, w_low = halves(weight[:, :RIM])
    high, low = halves(x)
    return mm(w_high, high) + mm(w_high, low) + mm(w_low, high)


def step_kernel(
    pot_in, tracer_in, u_in, v_in, w_in, geo_in, mass_hbm, dx_hbm, dy_hbm, col_hbm, cells_hbm, row_hbm, lane_hbm,
    out,
    mass_in, dx_in, dy_in, col_in, cells, cells_row, row_tab, lane_tab,
    xin, xc, mid, s1, s2, s3, s4, mgrid, rinv, mcol, kmat, inv,
    send1, recv0, recv1, send2, recv2, local, away, foreign, rim_inv,
    load_sem, send_sem, recv_sem,
):
    row = lax.axis_index("sfc")
    col = lax.axis_index("sub")
    n_row = lax.axis_size("sfc")
    n_col = lax.axis_size("sub")

    def device(side):
        return (lax.rem(row + side[0] + n_row, n_row), lax.rem(col + side[1] + n_col, n_col))

    barrier = pltpu.get_barrier_semaphore()
    for side in SIDES:
        pl.semaphore_signal(barrier, inc=1, device_id=device(side), device_id_type=MESH)

    sources = (geo_in, w_in, pot_in, tracer_in, u_in, v_in)
    loads = [pltpu.make_async_copy(ref, xin.at[k], load_sem.at[k]) for k, ref in enumerate(sources)]
    smalls = [
        pltpu.make_async_copy(source, place, load_sem.at[FIELDS + k])
        for k, (source, place) in enumerate(
            (
                (cells_hbm, cells), (cells_hbm, cells_row), (mass_hbm, mass_in), (dx_hbm, dx_in), (dy_hbm, dy_in),
                (col_hbm, col_in), (row_hbm, row_tab), (lane_hbm, lane_tab),
            )
        )
    ]
    for load in smalls + loads:
        load.start()

    def exchange(turn, send, recv, sides, start, counts, blocks=None, land=None):
        copies = []
        for k in sides:
            source, target = start[k], (land or start)[OPPOSITE[k]]
            lanes = pl.ds(0, send.shape[0]) if blocks is None else pl.ds(*blocks)
            copies.append(
                pltpu.make_async_remote_copy(
                    src_ref=send.at[lanes, pl.ds(source, counts[k])],
                    dst_ref=recv.at[lanes, pl.ds(target, counts[k])],
                    send_sem=send_sem.at[turn, k],
                    recv_sem=recv_sem.at[turn, OPPOSITE[k]],
                    device_id=device(SIDES[k]),
                    device_id_type=MESH,
                )
            )
        for copy in copies:
            copy.start()
        return copies

    for load in smalls:
        load.wait()

    def invert(c, carry):
        slot = jnp.int32(0)
        for j in range(TX * TY):
            slot = jnp.where(cells[0, j] == c, j, slot)
        inv[c] = slot
        return carry

    lax.fori_loop(0, TX * TY, invert, 0)

    dx = dx_in[...]
    dy = dy_in[...]
    deriv3 = weight3(jnp.concatenate([block_diag(dx, 3 * STRIP), block_diag(dy, 3 * STRIP)], axis=0))
    gather2 = onehot(node_point(iota((STRIP, 2 * STRIP), 0), iota((STRIP, 2 * STRIP), 1) % STRIP)).astype(BF16)
    spread2 = onehot(node_point(iota((STRIP, 2 * STRIP), 1) % STRIP, iota((STRIP, 2 * STRIP), 0))).astype(BF16)

    for send in (send1, local):
        send[...] = jnp.zeros_like(send)
    for grid in (s1, s2, s3, s4, mgrid):
        grid[:, 0:16] = jnp.zeros((grid.shape[0], 16, LEV), F32)

    def accumulate(grid, start, vals):
        head = pl.ds(start, 16)
        tail = pl.ds(pl.multiple_of(start + 16, 16), STRIP - 16)
        for k in range(grid.shape[0]):
            part = vals[:, k * LEV : (k + 1) * LEV]
            grid[k, head] = grid[k, head] + part[0:16]
            grid[k, tail] = part[16:]

    def scaled_strip(grid, here, inverse, count):
        return jnp.concatenate([grid[k, here] * inverse for k in range(count)], axis=1)

    def mass_strip(ey, carry):
        points = []
        for ex in range(TX):
            chosen = jnp.where(cells_row[...] == TX * ey + ex, mass_in[...], 0.0)
            points.append(jnp.broadcast_to(jnp.sum(chosen, axis=1, keepdims=True), (16, LEV)))
        strip_mass = jnp.concatenate(points, axis=0)
        mcol[pl.ds(pl.multiple_of(STRIP * ey, STRIP), STRIP)] = strip_mass
        accumulate(mgrid, pl.multiple_of(48 * ey, 16), mm(gather2, stack2(strip_mass)))
        return carry

    lax.fori_loop(0, TY, mass_strip, 0, unroll=True)
    gather_rim(mgrid, send1, (LINES, NEAR, FAR), range(1), 4)
    for load in loads:
        load.wait()

    def strip_of(ref, ey, fields):
        return jnp.concatenate([ref[k, pl.ds(TX * ey, TX)].reshape(STRIP, LEV) for k in fields], axis=1)

    def tend_strip(ey, carry):
        points = pl.ds(pl.multiple_of(STRIP * ey, STRIP), STRIP)
        for ex in range(TX):
            slot = inv[TX * ey + ex]
            for k in range(FIELDS):
                xc[k, TX * ey + ex] = xin[k, slot]
        x = strip_of(xc, ey, range(FIELDS))
        slopes = mm(deriv3, stack3(x[:, : 4 * LEV]))
        sx = slopes[:STRIP]
        sy = slopes[STRIP:]
        pot = x[:, 2 * LEV : 3 * LEV]
        u = x[:, 4 * LEV : 5 * LEV]
        v = x[:, 5 * LEV : 6 * LEV]

        def advect(k):
            cols = slice(k * LEV, (k + 1) * LEV)
            return -(u * sx[:, cols] + v * sy[:, cols])

        tend = [advect(2), advect(3), -sx[:, :LEV], -sy[:, :LEV], advect(1) + buoyancy * pot]
        weight = mcol[points]
        weighted = jnp.concatenate([t * weight for t in tend], axis=1)
        start = pl.multiple_of(48 * ey, 16)
        accumulate(s1, start, mm(gather2, stack2(weighted)))
        return carry

    lax.fori_loop(0, TY, tend_strip, 0, unroll=True)
    gather_rim(s1, send1, (LINES, NEAR, FAR), range(4))
    gather_rim(s1, send1, (LINES,), range(4, 5), 5)
    pl.semaphore_wait(barrier, 8)
    far_start = [first + n for first, n in zip(OFFSET, LINE_COUNT)]
    far_count = [n - m for m, n in zip(LINE_COUNT, FULL_COUNT)]
    line_copies = exchange(0, send1, recv0, DIRECT, OFFSET, LINE_COUNT, (0, 5), TURN_OFFSET)
    late_copies = exchange(1, send1, recv1, DIAGONAL, OFFSET, FULL_COUNT, (0, 5))
    late_copies += exchange(2, send1, recv1, DIRECT, far_start, far_count, (0, 5))

    col_high, col_low = halves(col_in[...])
    col3 = jnp.concatenate(
        [jnp.concatenate([col_high, col_low], axis=1), jnp.concatenate([col_high, jnp.zeros_like(col_low)], axis=1)],
        axis=0,
    )

    def newton(elements, which):
        change = {}
        for ey in sorted({ey for ey, _ in elements}):
            here = pl.ds(48 * ey, STRIP)
            change[ey] = mm(spread2, stack2(s1[4, here] * (rinv[which, here] * time_step)))
        for first in range(0, len(elements), 8):
            part = elements[first : first + 8]
            rows = [change[ey][16 * ex : 16 * ex + 16] + xc[1, TX * ey + ex] for ey, ex in part]
            geo = jnp.concatenate([xc[0, TX * ey + ex] for ey, ex in part], axis=0)
            target = geo + gravity_step * jnp.concatenate(rows, axis=0)
            phi = target
            lane = iota(phi.shape, 1)
            for _ in range(NEWTON):
                above = jnp.where(lane == LEV - 1, 0.0, pltpu.roll(phi, LEV - 1, 1))
                flux = jnp.tanh(above - phi)
                below = jnp.where(lane == 0, 0.0, pltpu.roll(flux, 1, 1))
                resid = phi - target - column_couple * (flux - below)
                step = mm(jnp.concatenate(halves(resid), axis=1), col3)
                phi = phi - (step[:, :LEV] + step[:, LEV:])
            for n, (ey, ex) in enumerate(part):
                mid[TX * ey + ex] = phi[16 * n : 16 * n + 16]

    lap = exact(dx, dx) + exact(dy, dy)
    lap_blk = block_diag(lap, 3 * STRIP)
    spread3 = onehot(node_point(iota((STRIP, 3 * STRIP), 1) % STRIP, iota((STRIP, 3 * STRIP), 0)))
    lap_nodes = exact(block_diag(lap, STRIP), spread3)

    def matrix_strip(ey, carry):
        strip_mass = mcol[pl.ds(pl.multiple_of(STRIP * ey, STRIP), STRIP)]
        wide = jnp.concatenate([strip_mass, strip_mass[:, :STRIP]], axis=1)
        kmat[0, ey] = weight3(mm(gather2, stack2(wide * lap_blk)))
        kmat[1, ey] = weight3(mm(gather2, stack2(wide * lap_nodes)))
        return carry

    lax.fori_loop(0, TY, matrix_strip, 0, unroll=True)

    def column(kind):
        return row_tab[:, kind : kind + 1]

    same_place = onehot(column(PLACE) == lane_tab[1][0:1, :RIM]).astype(BF16)

    def merge(x):
        high, low = halves(x)
        return mm(same_place, high) + mm(same_place, low)

    def reciprocal(total):
        return jnp.where(total > 0.0, 1.0 / jnp.where(total > 0.0, total, 1.0), 0.0)

    node_row = iota((NODES, LEV), 0) // PITCH
    node_col = iota((NODES, LEV), 0) % PITCH
    inside = (node_row > 0) & (node_row < ROWS - 1) & (node_col > 0) & (node_col < 12)
    rinv[1] = jnp.where(inside, reciprocal(mgrid[0]), 0.0)

    def first_strip(ey, carry):
        start = pl.multiple_of(48 * ey, 16)
        here = pl.ds(start, STRIP)
        rims = onehot((iota((STRIP, 2 * LEV), 0) + start).astype(F32) == lane_tab[0][0:1])
        nodal = jnp.concatenate([scaled_strip(s1, here, rinv[1, here] * time_step, 4), rims], axis=1)
        response = mm(kmat[1, ey], stack3(nodal))
        own = mm(kmat[0, ey], stack3(strip_of(xc, ey, (2, 3, 4, 5))))
        accumulate(s2, start, jnp.concatenate([response[:, : 4 * LEV] + own, response[:, 4 * LEV :]], axis=1))
        return carry

    lax.fori_loop(0, TY, first_strip, 0, unroll=True)
    gather_rim(s2, local, (LINES, NEAR), range(6))
    late_copies += exchange(3, local, away, DIRECT, OFFSET, NEAR_COUNT, (4, 2))
    late_copies += exchange(3, local, away, DIAGONAL, OFFSET, NEAR_COUNT, (0, 6))
    vert_copies = exchange(4, send1, recv1, DIRECT, OFFSET, LINE_COUNT, (5, 1))
    late_copies += exchange(4, send1, recv1, DIAGONAL, OFFSET, LINE_COUNT, (5, 1))

    def second_strip(ey, carry):
        start = pl.multiple_of(48 * ey, 16)
        here = pl.ds(start, STRIP)
        accumulate(s3, start, mm(kmat[1, ey], stack3(scaled_strip(s2, here, rinv[1, here], 6))))
        return carry

    lax.fori_loop(0, TY, second_strip, 0, unroll=True)
    gather_rim(s3, local, (LINES,), range(6), 6)
    late_copies += exchange(5, local, away, DIRECT, OFFSET, LINE_COUNT, (10, 2))
    late_copies += exchange(5, local, away, DIAGONAL, OFFSET, LINE_COUNT, (6, 6))

    newton([(ey, ex) for ey in range(1, TY - 1) for ex in (1, 2)], 1)

    def wide(x):
        return jnp.concatenate([x] * 4, axis=1)

    for copy in line_copies:
        copy.wait()
    edge = column(EDGE) > 0.0
    side_lines = spread_rows(
        [lanes_of(recv0, range(5))[first : first + rows] for first, rows in zip(TURN_OFFSET, TURN_ROWS)]
        + [jnp.zeros((16, 5 * LEV), F32)] * 4
    )
    edge_mass = jnp.where(edge, side_lines[:, 4 * LEV :] + send1[4], 1.0)
    edge_vals = jnp.where(edge, side_lines[:, : 4 * LEV] + lanes_of(send1, range(4)), 0.0)
    outer = swap_sides(edge_vals * wide(time_step / edge_mass))

    def send_turn(turn, vals):
        for k in range(4):
            for side in DIRECT:
                rows, start, first = TURN_ROWS[side], OFFSET[side], TURN_OFFSET[side]
                send2[turn, k, first : first + rows] = vals[start : start + rows, k * LEV : (k + 1) * LEV]
        counts = (NEAR_COUNT, LINE_COUNT)[turn]
        return exchange(6 + turn, send2.at[turn], recv2.at[turn], DIRECT, TURN_OFFSET, counts)

    turn_copies = send_turn(0, lanes_of(local, range(4)) + mm3(lanes_of(local, range(4, 6)), outer))
    turn_copies += send_turn(1, lanes_of(local, range(6, 10)) + mm3(lanes_of(local, range(10, 12)), outer))

    add_rim(mgrid, recv0.at[pl.ds(4, 1)], range(1), SIDE_LINES)
    rinv[0] = reciprocal(mgrid[0])
    for copy in vert_copies:
        copy.wait()
    for row, rows, start, stride in LINES[:4]:
        nodes = pl.ds(start, rows, stride=stride)
        s1[4, nodes] = s1[4, nodes] + recv1[5, row : row + rows]
    newton([(ey, ex) for ey in range(1, TY - 1) for ex in (0, 3)] + [(ey, ex) for ey in (0, TY - 1) for ex in (1, 2)], 0)

    for copy in late_copies:
        copy.wait()
    known = column(KNOWN) > 0.0
    line = column(LINE)
    unique = column(UNIQUE)
    side_line = (line > 0.0) & (column(SLOT) < 3.5)
    arrived_all = jnp.where(side_line, side_lines, jnp.where(known, lanes_of(recv1, range(5)), 0.0))
    arrived_all = arrived_all + unique * lanes_of(send1, range(5))
    totals = merge(arrived_all)
    rim_inv[...] = reciprocal(totals[:, 4 * LEV :])
    rim_state = totals[:, : 4 * LEV] * wide(rim_inv[...] * time_step)
    outer = swap_sides(unique * rim_state)
    own_block = column(SLOT) == lane_tab[2][0:1]
    rim_matrix = jnp.where(own_block & (column(CLOSE) > 0.0), lanes_of(away, range(4, 6)), 0.0)
    rim_matrix2 = jnp.where(own_block & (line > 0.0), lanes_of(away, range(10, 12)), 0.0)
    late = column(LATE) * rim_state
    diagonal = column(SLOT) > 3.5
    late_one = mm3(rim_matrix, late) + jnp.where(diagonal & (column(CLOSE) > 0.0), lanes_of(away, range(4)), 0.0)
    late_two = mm3(rim_matrix2, late) + jnp.where(diagonal & (line > 0.0), lanes_of(away, range(6, 10)), 0.0)
    add_rim(mgrid, recv1.at[pl.ds(4, 1)], range(1), CORNER_LINES)
    rinv[0] = reciprocal(mgrid[0])
    add_rim(s1, recv0, range(4), SIDE_LINES)
    add_rim(s1, recv1, range(4), CORNER_LINES)
    for row, rows, start, stride in CORNER_LINES:
        nodes = pl.ds(start, rows, stride=stride)
        s1[4, nodes] = s1[4, nodes] + recv1[5, row : row + rows]
    newton([(ey, ex) for ey in (0, TY - 1) for ex in (0, 3)], 0)

    rim_nodes = lanes_of(s2, range(4, 6))
    own_sum = lanes_of(local, range(4)) + mm3(lanes_of(local, range(4, 6)), outer)
    own_rim = jnp.where(line > 0.0, own_sum, 0.0) * wide(rim_inv[...])
    again = lanes_of(s3, range(4)) + mm3(lanes_of(s3, range(4, 6)), outer)
    for k in range(4):
        s4[k] = again[:, k * LEV : (k + 1) * LEV]

    def place_column(j, carry):
        phi = mid[cells[0, j]]
        out[5, j] = phi
        out[4, j] = (phi - xc[0, cells[0, j]]) / gravity_step
        return carry

    lax.fori_loop(0, TX * TY, place_column, 0, unroll=True)

    inverse = rim_inv[...]

    def received(part, counts):
        def rows(k, side):
            first = TURN_OFFSET[side]
            return recv2[part, k, first : first + counts[side]]

        return jnp.concatenate(
            [
                spread_rows([rows(k, side) for side in range(4)] + [jnp.zeros((16, LEV), F32)] * 4)
                for k in range(4)
            ],
            axis=1,
        )

    for copy in turn_copies:
        copy.wait()
    direct = ~diagonal
    first_turn = jnp.where(direct & (column(CLOSE) > 0.0), received(0, TURN_ROWS), 0.0) + late_one
    arrived = merge(first_turn) * wide(inverse)
    turned = jnp.where(direct & (line > 0.0), received(1, TURN_ROWS), 0.0) + late_two
    outside = mm3(rim_matrix, arrived + own_rim) + turned
    inner = mm3(rim_nodes, swap_sides((arrived + own_rim) * unique))
    for k in range(4):
        foreign[k] = outside[:, k * LEV : (k + 1) * LEV]
        s4[k] = s4[k] + inner[:, k * LEV : (k + 1) * LEV]
    add_rim(s4, foreign, range(4))

    def final_strip(ey, carry):
        here = pl.ds(pl.multiple_of(48 * ey, 16), STRIP)
        inverse = rinv[0, here]
        nodal = jnp.concatenate(
            [(time_step * s1[k, here] - visc_coef * s4[k, here]) * inverse for k in range(4)], axis=1
        )
        final = strip_of(xc, ey, (2, 3, 4, 5)) + mm(spread2, stack2(nodal))
        for k in range(4):
            xc[2 + k, pl.ds(TX * ey, TX)] = final[:, k * LEV : (k + 1) * LEV].reshape(TX, 16, LEV)
        return carry

    lax.fori_loop(0, TY, final_strip, 0, unroll=True)

    def place_fields(j, carry):
        for k in range(4):
            out[k, j] = xc[2 + k, cells[0, j]]
        return carry

    lax.fori_loop(0, TX * TY, place_fields, 0, unroll=True)


def store_kernel(fields, *refs):
    outs, sem = refs[:FIELDS], refs[FIELDS]
    copies = [pltpu.make_async_copy(fields.at[k], outs[k], sem.at[k]) for k in range(FIELDS)]
    for copy in copies:
        copy.start()
    for copy in copies:
        copy.wait()


def per_device(pot_temp, tracer, wind_u, wind_v, vert_w, geopot, elem_mass, deriv_x, deriv_y, col_inverse, element_cell):
    shape = pot_temp.shape
    vmem = pl.BlockSpec(memory_space=pltpu.VMEM)
    hbm = pl.BlockSpec(memory_space=pl.ANY)
    rows, lanes = rim_tables()
    fields = pl.pallas_call(
        step_kernel,
        out_shape=pltpu.VMEM((FIELDS,) + shape, F32),
        in_specs=[hbm] * 13,
        out_specs=vmem,
        scratch_shapes=[
            pltpu.VMEM((16, TX * TY), F32),
            pltpu.VMEM((16, 16), F32),
            pltpu.VMEM((16, 16), F32),
            pltpu.VMEM((LEV, LEV), F32),
            pltpu.SMEM((1, TX * TY), jnp.int32),
            pltpu.VMEM((1, TX * TY), jnp.int32),
            pltpu.VMEM(rows.shape, F32),
            pltpu.VMEM(lanes.shape, F32),
            pltpu.VMEM((FIELDS,) + shape, F32),
            pltpu.VMEM((FIELDS,) + shape, F32),
            pltpu.VMEM(shape, F32),
            pltpu.VMEM((5, NODES, LEV), F32),
            pltpu.VMEM((6, NODES, LEV), F32),
            pltpu.VMEM((6, NODES, LEV), F32),
            pltpu.VMEM((4, NODES, LEV), F32),
            pltpu.VMEM((1, NODES, LEV), F32),
            pltpu.VMEM((2, NODES, LEV), F32),
            pltpu.VMEM((512, LEV), F32),
            pltpu.VMEM((2, TY, STRIP, 3 * STRIP), BF16),
            pltpu.SMEM((TX * TY,), jnp.int32),
        ]
        + [pltpu.VMEM((6, RIM, LEV), F32), pltpu.VMEM((5, TURN_RIM, LEV), F32), pltpu.VMEM((6, RIM, LEV), F32)]
        + [pltpu.VMEM((2, 4, TURN_RIM, LEV), F32)] * 2
        + [pltpu.VMEM((blocks, RIM, LEV), F32) for blocks in (12, 12, 4)]
        + [
            pltpu.VMEM((RIM, LEV), F32),
            pltpu.SemaphoreType.DMA((FIELDS + 8,)),
            pltpu.SemaphoreType.DMA((8, 8)),
            pltpu.SemaphoreType.DMA((8, 8)),
        ],
        compiler_params=pltpu.CompilerParams(collective_id=0, has_side_effects=True, vmem_limit_bytes=62 << 20),
    )(pot_temp, tracer, wind_u, wind_v, vert_w, geopot, elem_mass.T, deriv_x, deriv_y, col_inverse, element_cell, rows, lanes)
    result = jax.ShapeDtypeStruct(shape, F32)
    return tuple(
        pl.pallas_call(
            store_kernel,
            out_shape=[result] * FIELDS,
            in_specs=[vmem],
            out_specs=[hbm] * FIELDS,
            scratch_shapes=[pltpu.SemaphoreType.DMA((FIELDS,))],
            compiler_params=pltpu.CompilerParams(vmem_limit_bytes=48 << 20),
        )(fields)
    )


def solution(mesh):
    field = P(("sfc", "sub"), None, None)
    flat = P(("sfc", "sub"), None)
    return jax.shard_map(
        per_device,
        mesh=mesh,
        in_specs=(field,) * 6 + (flat, P(), P(), P(), flat),
        out_specs=(field,) * 6,
        check_vma=False,
    )
```

```python
import jax
import jax.numpy as jnp
import numpy as np
from jax import lax
from jax.experimental import pallas as pl
from jax.experimental.pallas import tpu as pltpu
from jax.sharding import PartitionSpec as P

TX = 4
TY = 8
LEV = 128
NEWTON = 3
PITCH = 16
ROWS = 3 * TY + 1
NODES = ROWS * PITCH
STRIP = 64
FIELDS = 6

time_step = 0.4
visc_coef = 0.1
buoyancy = 0.5
gravity_step = 0.5
column_couple = 0.25

F32 = jnp.float32
BF16 = jnp.bfloat16
MESH = pl.DeviceIdType.MESH

SIDES = ((0, -1), (0, 1), (-1, 0), (1, 0), (-1, -1), (-1, 1), (1, -1), (1, 1))
OPPOSITE = (1, 0, 3, 2, 7, 6, 5, 4)
OFFSET = (0, 40, 80, 112, 144, 160, 176, 192)
COUNT = (40, 40, 32, 32, 16, 16, 16, 16)
RIM = 208
LINE_COUNT = (25, 25, 13, 13, 1, 1, 1, 1)
NEAR_COUNT = (31, 31, 19, 19, 7, 7, 7, 7)
FULL_COUNT = (37, 37, 25, 25, 13, 13, 13, 13)
DIRECT = (2, 3, 0, 1)
DIAGONAL = (4, 5, 6, 7)
TURN_ROWS = (32, 32, 24, 24)
TURN_OFFSET = (0, 32, 64, 88)
TURN_RIM = 112
LINES = (
    (0, 25, 0, 16), (40, 25, 12, 16), (80, 13, 0, 1), (112, 13, 384, 1),
    (144, 1, 0, 1), (160, 1, 12, 1), (176, 1, 384, 1), (192, 1, 396, 1),
)
NEAR = (
    (25, 3, 1, 1), (28, 3, 385, 1), (65, 3, 9, 1), (68, 3, 393, 1),
    (93, 3, 16, 16), (96, 3, 28, 16), (125, 3, 336, 16), (128, 3, 348, 16),
    (145, 3, 1, 1), (148, 3, 16, 16), (161, 3, 9, 1), (164, 3, 28, 16),
    (177, 3, 385, 1), (180, 3, 336, 16), (193, 3, 393, 1), (196, 3, 348, 16),
)
FAR = (
    (31, 3, 4, 1), (34, 3, 388, 1), (71, 3, 6, 1), (74, 3, 390, 1),
    (99, 3, 64, 16), (102, 3, 76, 16), (131, 3, 288, 16), (134, 3, 300, 16),
    (151, 3, 4, 1), (154, 3, 64, 16), (167, 3, 6, 1), (170, 3, 76, 16),
    (183, 3, 388, 1), (186, 3, 288, 16), (199, 3, 390, 1), (202, 3, 300, 16),
)
SIDE_LINES = ((0, 25, 0, 16), (32, 25, 12, 16), (64, 13, 0, 1), (88, 13, 384, 1))
CORNER_LINES = LINES[4:]
PLACE, KNOWN, LINE, UNIQUE, EDGE, LATE, CLOSE, SLOT = range(8)


def rim_tables():
    node = np.full(RIM, -1)
    line = np.zeros(RIM)
    close = np.zeros(RIM)
    for group in (LINES, NEAR, FAR):
        for first, rows, start, stride in group:
            node[first : first + rows] = start + stride * np.arange(rows)
            line[first : first + rows] = group is LINES
            close[first : first + rows] = group is not FAR
    place = np.arange(RIM) - 4000.0
    slot = np.zeros(RIM)
    lane_node = np.full(RIM, -1)
    for k in range(8):
        mine = np.arange(OFFSET[k], OFFSET[k] + COUNT[k])
        theirs = mine - OFFSET[k] + OFFSET[OPPOSITE[k]]
        slot[mine] = k
        lane_node[mine] = node[theirs]
        known = node[theirs] >= 0
        ny = node[theirs] // PITCH + 3 * TY * SIDES[k][0]
        nx = node[theirs] % PITCH + 3 * TX * SIDES[k][1]
        place[mine[known]] = ((ny + 8) * 64 + nx + 8)[known]
    corner = np.zeros(RIM)
    corner[[0, 24, 40, 64, 80, 92, 112, 124]] = 1
    unique = line * (slot < 4) * np.where(slot < 2, 1, 1 - corner)
    edge = line * (slot < 4) * (1 - corner)
    late = np.where(slot < 4, corner, node >= 0)
    rows = np.zeros((RIM, LEV))
    for column, table in enumerate((place, node >= 0, line, unique, edge, late, close, slot)):
        rows[:, column] = table
    lanes = np.full((3, 8, 2 * LEV), -9000.0)
    lanes[:, :, :RIM] = np.stack([lane_node, place, slot])[:, None]
    return rows.astype(np.float32), lanes.astype(np.float32)


def iota(shape, dim):
    return lax.broadcasted_iota(jnp.int32, shape, dim)


def halves(x):
    high = x.astype(BF16)
    return high, (x - high.astype(F32)).astype(BF16)


def stack2(x):
    high, low = halves(x)
    return jnp.concatenate([high, low], axis=0)


def stack3(x):
    high, low = halves(x)
    return jnp.concatenate([high, low, high], axis=0)


def weight3(x):
    high, low = halves(x)
    return jnp.where(iota(x.shape, 1) < 2 * (x.shape[1] // 3), high.astype(F32), low.astype(F32)).astype(BF16)


def mm(a, b):
    return jnp.dot(a, b, preferred_element_type=F32)


def exact(a, b):
    return jnp.dot(a, b, preferred_element_type=F32, precision=lax.Precision.HIGHEST)


def onehot(cond):
    return jnp.where(cond, 1.0, 0.0).astype(F32)


def block_diag(matrix, cols):
    left = onehot(iota((STRIP, 16), 0) % 16 == iota((STRIP, 16), 1))
    right = onehot(iota((16, cols), 1) % 16 == iota((16, cols), 0))
    spread = exact(exact(left, matrix), right)
    same = (iota((STRIP, cols), 1) % STRIP) // 16 == iota((STRIP, cols), 0) // 16
    return jnp.where(same, spread, 0.0)


def node_point(node, point):
    return (node // PITCH == (point % 16) // 4) & (node % PITCH == 3 * (point // 16) + point % 4)


def gather_rim(grid, send, groups, blocks, first=0):
    for n, k in enumerate(blocks):
        for group in groups:
            for row, rows, start, stride in group:
                send[first + n, row : row + rows] = grid[k, pl.ds(start, rows, stride=stride)]


def add_rim(grid, recv, blocks, lines=LINES):
    for k in blocks:
        for row, rows, start, stride in lines:
            nodes = pl.ds(start, rows, stride=stride)
            grid[k, nodes] = grid[k, nodes] + recv[k, row : row + rows]


def lanes_of(ref, blocks):
    return jnp.concatenate([ref[k] for k in blocks], axis=1)


def spread_rows(parts):
    filled = []
    for k, part in enumerate(parts):
        filled.append(part)
        if part.shape[0] < COUNT[k]:
            filled.append(jnp.zeros((COUNT[k] - part.shape[0], part.shape[1]), F32))
    return jnp.concatenate(filled, axis=0)


def swap_sides(x):
    return jnp.concatenate([x[OFFSET[k] : OFFSET[k] + COUNT[k]] for k in OPPOSITE], axis=0)


def mm3(weight, x):
    w_high, w_low = weight if isinstance(weight, tuple) else halves(weight[:, :RIM])
    high, low = halves(x)
    return mm(w_high, high) + mm(w_high, low) + mm(w_low, high)


def step_kernel(
    pot_in, tracer_in, u_in, v_in, w_in, geo_in, mass_hbm, dx_hbm, dy_hbm, col_hbm, cells_hbm, row_hbm, lane_hbm,
    out,
    mass_in, dx_in, dy_in, col_in, cells, cells_row, row_tab, lane_tab,
    xin, xc, mid, s1, s2, s3, s4, mgrid, rinv, mcol, kmat, inv,
    send1, recv0, recv1, recv_vert, local, away, foreign, rim_inv,
    load_sem, send_sem, recv_sem,
):
    row = lax.axis_index("sfc")
    col = lax.axis_index("sub")
    n_row = lax.axis_size("sfc")
    n_col = lax.axis_size("sub")

    def device(side):
        return (lax.rem(row + side[0] + n_row, n_row), lax.rem(col + side[1] + n_col, n_col))

    barrier = pltpu.get_barrier_semaphore()
    for side in SIDES:
        pl.semaphore_signal(barrier, inc=1, device_id=device(side), device_id_type=MESH)

    sources = (geo_in, w_in, pot_in, tracer_in, u_in, v_in)
    loads = [pltpu.make_async_copy(ref, xin.at[k], load_sem.at[k]) for k, ref in enumerate(sources)]
    smalls = [
        pltpu.make_async_copy(source, place, load_sem.at[FIELDS + k])
        for k, (source, place) in enumerate(
            (
                (cells_hbm, cells), (cells_hbm, cells_row), (mass_hbm, mass_in), (dx_hbm, dx_in), (dy_hbm, dy_in),
                (col_hbm, col_in), (row_hbm, row_tab), (lane_hbm, lane_tab),
            )
        )
    ]
    for load in smalls + loads:
        load.start()

    def exchange(turn, send, recv, sides, start, counts, blocks=None, land=None):
        copies = []
        for k in sides:
            source, target = start[k], (land or start)[OPPOSITE[k]]
            lanes = pl.ds(0, send.shape[0]) if blocks is None else pl.ds(*blocks)
            copies.append(
                pltpu.make_async_remote_copy(
                    src_ref=send.at[lanes, pl.ds(source, counts[k])],
                    dst_ref=recv.at[lanes, pl.ds(target, counts[k])],
                    send_sem=send_sem.at[turn, k],
                    recv_sem=recv_sem.at[turn, OPPOSITE[k]],
                    device_id=device(SIDES[k]),
                    device_id_type=MESH,
                )
            )
        for copy in copies:
            copy.start()
        return copies

    for load in smalls:
        load.wait()

    def invert(c, carry):
        slot = jnp.int32(0)
        for j in range(TX * TY):
            slot = jnp.where(cells[0, j] == c, j, slot)
        inv[c] = slot
        return carry

    lax.fori_loop(0, TX * TY, invert, 0)

    dx = dx_in[...]
    dy = dy_in[...]
    deriv3 = weight3(jnp.concatenate([block_diag(dx, 3 * STRIP), block_diag(dy, 3 * STRIP)], axis=0))
    gather2 = onehot(node_point(iota((STRIP, 2 * STRIP), 0), iota((STRIP, 2 * STRIP), 1) % STRIP)).astype(BF16)
    spread2 = onehot(node_point(iota((STRIP, 2 * STRIP), 1) % STRIP, iota((STRIP, 2 * STRIP), 0))).astype(BF16)

    for send in (send1, local):
        send[...] = jnp.zeros_like(send)
    for grid in (s1, s2, s3, s4, mgrid):
        grid[:, 0:16] = jnp.zeros((grid.shape[0], 16, LEV), F32)

    def accumulate(grid, start, vals):
        head = pl.ds(start, 16)
        tail = pl.ds(pl.multiple_of(start + 16, 16), STRIP - 16)
        for k in range(grid.shape[0]):
            part = vals[:, k * LEV : (k + 1) * LEV]
            grid[k, head] = grid[k, head] + part[0:16]
            grid[k, tail] = part[16:]

    def scaled_strip(grid, here, inverse, count):
        return jnp.concatenate([grid[k, here] * inverse for k in range(count)], axis=1)

    def mass_strip(ey, carry):
        points = []
        for ex in range(TX):
            chosen = jnp.where(cells_row[...] == TX * ey + ex, mass_in[...], 0.0)
            points.append(jnp.broadcast_to(jnp.sum(chosen, axis=1, keepdims=True), (16, LEV)))
        strip_mass = jnp.concatenate(points, axis=0)
        mcol[pl.ds(pl.multiple_of(STRIP * ey, STRIP), STRIP)] = strip_mass
        accumulate(mgrid, pl.multiple_of(48 * ey, 16), mm(gather2, stack2(strip_mass)))
        return carry

    lax.fori_loop(0, TY, mass_strip, 0, unroll=True)
    gather_rim(mgrid, send1, (LINES, NEAR, FAR), range(1), 1)
    for load in loads:
        load.wait()

    def strip_of(ref, ey, fields):
        return jnp.concatenate([ref[k, pl.ds(TX * ey, TX)].reshape(STRIP, LEV) for k in fields], axis=1)

    def tend_strip(ey, carry):
        points = pl.ds(pl.multiple_of(STRIP * ey, STRIP), STRIP)
        for ex in range(TX):
            slot = inv[TX * ey + ex]
            for k in range(FIELDS):
                xc[k, TX * ey + ex] = xin[k, slot]
        x = strip_of(xc, ey, range(FIELDS))
        slopes = mm(deriv3, stack3(x[:, : 4 * LEV]))
        sx = slopes[:STRIP]
        sy = slopes[STRIP:]
        pot = x[:, 2 * LEV : 3 * LEV]
        u = x[:, 4 * LEV : 5 * LEV]
        v = x[:, 5 * LEV : 6 * LEV]

        def advect(k):
            cols = slice(k * LEV, (k + 1) * LEV)
            return -(u * sx[:, cols] + v * sy[:, cols])

        tend = [advect(2), advect(3), -sx[:, :LEV], -sy[:, :LEV], advect(1) + buoyancy * pot]
        weight = mcol[points]
        weighted = jnp.concatenate([t * weight for t in tend], axis=1)
        start = pl.multiple_of(48 * ey, 16)
        accumulate(s1, start, mm(gather2, stack2(weighted)))
        return carry

    lax.fori_loop(0, TY, tend_strip, 0, unroll=True)
    gather_rim(s1, send1, (LINES,), range(4, 5), 0)
    gather_rim(s1, send1, (LINES, NEAR, FAR), range(4), 2)
    pl.semaphore_wait(barrier, 8)
    far_start = [first + n for first, n in zip(OFFSET, LINE_COUNT)]
    far_count = [n - m for m, n in zip(LINE_COUNT, FULL_COUNT)]
    vert_copies = exchange(4, send1, recv_vert, range(8), OFFSET, LINE_COUNT, (0, 2))
    line_copies = exchange(0, send1, recv0, DIRECT, OFFSET, LINE_COUNT, (2, 4), TURN_OFFSET)
    line_copies += exchange(1, send1, recv1, DIAGONAL, OFFSET, FULL_COUNT, (1, 5))
    line_copies += exchange(2, send1, recv1, DIRECT, far_start, far_count, (1, 5))

    col_high, col_low = halves(col_in[...])
    col3 = jnp.concatenate(
        [jnp.concatenate([col_high, col_low], axis=1), jnp.concatenate([col_high, jnp.zeros_like(col_low)], axis=1)],
        axis=0,
    )

    def newton(elements, which):
        change = {}
        for ey in sorted({ey for ey, _ in elements}):
            here = pl.ds(48 * ey, STRIP)
            change[ey] = mm(spread2, stack2(s1[4, here] * (rinv[which, here] * time_step)))
        for first in range(0, len(elements), 20):
            part = elements[first : first + 20]
            rows = [change[ey][16 * ex : 16 * ex + 16] + xc[1, TX * ey + ex] for ey, ex in part]
            geo = jnp.concatenate([xc[0, TX * ey + ex] for ey, ex in part], axis=0)
            target = geo + gravity_step * jnp.concatenate(rows, axis=0)
            phi = target
            lane = iota(phi.shape, 1)
            for _ in range(NEWTON):
                above = jnp.where(lane == LEV - 1, 0.0, pltpu.roll(phi, LEV - 1, 1))
                flux = jnp.tanh(above - phi)
                below = jnp.where(lane == 0, 0.0, pltpu.roll(flux, 1, 1))
                resid = phi - target - column_couple * (flux - below)
                step = mm(jnp.concatenate(halves(resid), axis=1), col3)
                phi = phi - (step[:, :LEV] + step[:, LEV:])
            for n, (ey, ex) in enumerate(part):
                mid[TX * ey + ex] = phi[16 * n : 16 * n + 16]

    lap = exact(dx, dx) + exact(dy, dy)
    lap_blk = block_diag(lap, 3 * STRIP)
    spread3 = onehot(node_point(iota((STRIP, 3 * STRIP), 1) % STRIP, iota((STRIP, 3 * STRIP), 0)))
    lap_nodes = exact(block_diag(lap, STRIP), spread3)

    def matrix_strip(ey, carry):
        strip_mass = mcol[pl.ds(pl.multiple_of(STRIP * ey, STRIP), STRIP)]
        wide = jnp.concatenate([strip_mass, strip_mass[:, :STRIP]], axis=1)
        kmat[0, ey] = weight3(mm(gather2, stack2(wide * lap_blk)))
        kmat[1, ey] = weight3(mm(gather2, stack2(wide * lap_nodes)))
        return carry

    lax.fori_loop(0, TY, matrix_strip, 0, unroll=True)

    def column(kind):
        return row_tab[:, kind : kind + 1]

    same_place = onehot(column(PLACE) == lane_tab[1][0:1, :RIM]).astype(BF16)

    def merge(x):
        high, low = halves(x)
        return mm(same_place, high) + mm(same_place, low)

    def reciprocal(total):
        return jnp.where(total > 0.0, 1.0 / jnp.where(total > 0.0, total, 1.0), 0.0)

    node_row = iota((NODES, LEV), 0) // PITCH
    node_col = iota((NODES, LEV), 0) % PITCH
    inside = (node_row > 0) & (node_row < ROWS - 1) & (node_col > 0) & (node_col < 12)
    rinv[1] = jnp.where(inside, reciprocal(mgrid[0]), 0.0)

    def first_strip(ey, carry):
        start = pl.multiple_of(48 * ey, 16)
        here = pl.ds(start, STRIP)
        rims = onehot((iota((STRIP, 2 * LEV), 0) + start).astype(F32) == lane_tab[0][0:1])
        nodal = jnp.concatenate([scaled_strip(s1, here, rinv[1, here] * time_step, 4), rims], axis=1)
        response = mm(kmat[1, ey], stack3(nodal))
        own = mm(kmat[0, ey], stack3(strip_of(xc, ey, (2, 3, 4, 5))))
        accumulate(s2, start, jnp.concatenate([response[:, : 4 * LEV] + own, response[:, 4 * LEV :]], axis=1))
        return carry

    lax.fori_loop(0, TY, first_strip, 0, unroll=True)
    gather_rim(s2, local, (LINES, NEAR), range(6))
    near_copies = exchange(3, local, away, range(8), OFFSET, NEAR_COUNT, (0, 6))

    def second_strip(ey, carry):
        start = pl.multiple_of(48 * ey, 16)
        here = pl.ds(start, STRIP)
        accumulate(s3, start, mm(kmat[1, ey], stack3(scaled_strip(s2, here, rinv[1, here], 6))))
        return carry

    lax.fori_loop(0, TY, second_strip, 0, unroll=True)
    gather_rim(s3, local, (LINES,), range(6), 6)
    far_copies = exchange(5, local, away, range(8), OFFSET, LINE_COUNT, (6, 6))

    own_weight = halves(lanes_of(local, range(4, 6))[:, :RIM])
    again_weight = halves(lanes_of(s3, range(4, 6))[:, :RIM])
    inner_weight = halves(lanes_of(s2, range(4, 6))[:, :RIM])
    newton([(ey, ex) for ey in range(1, TY - 1) for ex in (1, 2)], 1)

    def wide(x):
        return jnp.concatenate([x] * 4, axis=1)

    known = column(KNOWN) > 0.0
    line = column(LINE)
    unique = column(UNIQUE)
    side_line = (line > 0.0) & (column(SLOT) < 3.5)
    own_block = column(SLOT) == lane_tab[2][0:1]
    close = column(CLOSE) > 0.0

    for copy in vert_copies:
        copy.wait()
    add_rim(mgrid, recv_vert.at[pl.ds(1, 1)], range(1))
    rinv[0] = reciprocal(mgrid[0])
    for row, rows, start, stride in LINES:
        nodes = pl.ds(start, rows, stride=stride)
        s1[4, nodes] = s1[4, nodes] + recv_vert[0, row : row + rows]
    newton(
        [(ey, ex) for ey in range(1, TY - 1) for ex in (0, 3)] + [(ey, ex) for ey in (0, TY - 1) for ex in range(TX)], 0
    )

    for copy in line_copies:
        copy.wait()
    side_lines = spread_rows(
        [lanes_of(recv0, range(2, 6))[first : first + rows] for first, rows in zip(TURN_OFFSET, TURN_ROWS)]
        + [jnp.zeros((16, 4 * LEV), F32)] * 4
    )
    arrived_all = jnp.where(side_line, side_lines, jnp.where(known, lanes_of(recv1, range(2, 6)), 0.0))
    mass_all = jnp.where(line > 0.0, recv_vert[1], jnp.where(known, recv1[1], 0.0))
    rim_inv[...] = reciprocal(merge(mass_all + unique * send1[1]))
    totals = merge(arrived_all + unique * lanes_of(send1, range(2, 6)))
    rim_state = totals * wide(rim_inv[...] * time_step)
    outer = swap_sides(unique * rim_state)
    for k in range(4):
        for row, rows, start, stride in SIDE_LINES:
            nodes = pl.ds(start, rows, stride=stride)
            s1[k, nodes] = s1[k, nodes] + recv0[2 + k, row : row + rows]
        for row, rows, start, stride in CORNER_LINES:
            nodes = pl.ds(start, rows, stride=stride)
            s1[k, nodes] = s1[k, nodes] + recv1[2 + k, row : row + rows]
    own_sum = lanes_of(local, range(4)) + mm3(own_weight, outer)
    own_rim = jnp.where(line > 0.0, own_sum, 0.0) * wide(rim_inv[...])
    again = lanes_of(s3, range(4)) + mm3(again_weight, outer)
    for k in range(4):
        s4[k] = again[:, k * LEV : (k + 1) * LEV]

    def place_column(j, carry):
        phi = mid[cells[0, j]]
        out[5, j] = phi
        out[4, j] = (phi - xc[0, cells[0, j]]) / gravity_step
        return carry

    lax.fori_loop(0, TX * TY, place_column, 0, unroll=True)

    inverse = rim_inv[...]
    for copy in near_copies:
        copy.wait()
    rim_matrix = jnp.where(own_block & close, lanes_of(away, range(4, 6)), 0.0)
    first_turn = jnp.where(close, lanes_of(away, range(4)), 0.0) + mm3(rim_matrix, rim_state)
    rim_next = merge(first_turn) * wide(inverse) + own_rim
    outside = mm3(rim_matrix, rim_next)
    inner = mm3(inner_weight, swap_sides(rim_next * unique))
    for copy in far_copies:
        copy.wait()
    rim_matrix2 = jnp.where(own_block & (line > 0.0), lanes_of(away, range(10, 12)), 0.0)
    outside = outside + jnp.where(line > 0.0, lanes_of(away, range(6, 10)), 0.0) + mm3(rim_matrix2, rim_state)
    for k in range(4):
        foreign[k] = outside[:, k * LEV : (k + 1) * LEV]
        s4[k] = s4[k] + inner[:, k * LEV : (k + 1) * LEV]
    add_rim(s4, foreign, range(4))

    def final_strip(ey, carry):
        here = pl.ds(pl.multiple_of(48 * ey, 16), STRIP)
        inverse = rinv[0, here]
        nodal = jnp.concatenate(
            [(time_step * s1[k, here] - visc_coef * s4[k, here]) * inverse for k in range(4)], axis=1
        )
        final = strip_of(xc, ey, (2, 3, 4, 5)) + mm(spread2, stack2(nodal))
        for k in range(4):
            xc[2 + k, pl.ds(TX * ey, TX)] = final[:, k * LEV : (k + 1) * LEV].reshape(TX, 16, LEV)
        return carry

    lax.fori_loop(0, TY, final_strip, 0, unroll=True)

    def place_fields(j, carry):
        for k in range(4):
            out[k, j] = xc[2 + k, cells[0, j]]
        return carry

    lax.fori_loop(0, TX * TY, place_fields, 0, unroll=True)


def store_kernel(fields, *refs):
    outs, sem = refs[:FIELDS], refs[FIELDS]
    copies = [pltpu.make_async_copy(fields.at[k], outs[k], sem.at[k]) for k in range(FIELDS)]
    for copy in copies:
        copy.start()
    for copy in copies:
        copy.wait()


def per_device(pot_temp, tracer, wind_u, wind_v, vert_w, geopot, elem_mass, deriv_x, deriv_y, col_inverse, element_cell):
    shape = pot_temp.shape
    vmem = pl.BlockSpec(memory_space=pltpu.VMEM)
    hbm = pl.BlockSpec(memory_space=pl.ANY)
    rows, lanes = rim_tables()
    fields = pl.pallas_call(
        step_kernel,
        out_shape=pltpu.VMEM((FIELDS,) + shape, F32),
        in_specs=[hbm] * 13,
        out_specs=vmem,
        scratch_shapes=[
            pltpu.VMEM((16, TX * TY), F32),
            pltpu.VMEM((16, 16), F32),
            pltpu.VMEM((16, 16), F32),
            pltpu.VMEM((LEV, LEV), F32),
            pltpu.SMEM((1, TX * TY), jnp.int32),
            pltpu.VMEM((1, TX * TY), jnp.int32),
            pltpu.VMEM(rows.shape, F32),
            pltpu.VMEM(lanes.shape, F32),
            pltpu.VMEM((FIELDS,) + shape, F32),
            pltpu.VMEM((FIELDS,) + shape, F32),
            pltpu.VMEM(shape, F32),
            pltpu.VMEM((5, NODES, LEV), F32),
            pltpu.VMEM((6, NODES, LEV), F32),
            pltpu.VMEM((6, NODES, LEV), F32),
            pltpu.VMEM((4, NODES, LEV), F32),
            pltpu.VMEM((1, NODES, LEV), F32),
            pltpu.VMEM((2, NODES, LEV), F32),
            pltpu.VMEM((512, LEV), F32),
            pltpu.VMEM((2, TY, STRIP, 3 * STRIP), BF16),
            pltpu.SMEM((TX * TY,), jnp.int32),
        ]
        + [pltpu.VMEM((6, RIM, LEV), F32), pltpu.VMEM((6, TURN_RIM, LEV), F32), pltpu.VMEM((6, RIM, LEV), F32)]
        + [pltpu.VMEM((2, RIM, LEV), F32)]
        + [pltpu.VMEM((blocks, RIM, LEV), F32) for blocks in (12, 12, 4)]
        + [
            pltpu.VMEM((RIM, LEV), F32),
            pltpu.SemaphoreType.DMA((FIELDS + 8,)),
            pltpu.SemaphoreType.DMA((6, 8)),
            pltpu.SemaphoreType.DMA((6, 8)),
        ],
        compiler_params=pltpu.CompilerParams(collective_id=0, has_side_effects=True, vmem_limit_bytes=62 << 20),
    )(pot_temp, tracer, wind_u, wind_v, vert_w, geopot, elem_mass.T, deriv_x, deriv_y, col_inverse, element_cell, rows, lanes)
    result = jax.ShapeDtypeStruct(shape, F32)
    return tuple(
        pl.pallas_call(
            store_kernel,
            out_shape=[result] * FIELDS,
            in_specs=[vmem],
            out_specs=[hbm] * FIELDS,
            scratch_shapes=[pltpu.SemaphoreType.DMA((FIELDS,))],
            compiler_params=pltpu.CompilerParams(vmem_limit_bytes=48 << 20),
        )(fields)
    )


def solution(mesh):
    field = P(("sfc", "sub"), None, None)
    flat = P(("sfc", "sub"), None)
    return jax.shard_map(
        per_device,
        mesh=mesh,
        in_specs=(field,) * 6 + (flat, P(), P(), P(), flat),
        out_specs=(field,) * 6,
        check_vma=False,
    )
```

```python
import jax
import jax.numpy as jnp
import numpy as np
from jax import lax
from jax.experimental import pallas as pl
from jax.experimental.pallas import tpu as pltpu
from jax.sharding import PartitionSpec as P

TX = 4
TY = 8
LEV = 128
NEWTON = 3
PITCH = 16
ROWS = 3 * TY + 1
NODES = ROWS * PITCH
STRIP = 64
FIELDS = 6

time_step = 0.4
visc_coef = 0.1
buoyancy = 0.5
gravity_step = 0.5
column_couple = 0.25

F32 = jnp.float32
BF16 = jnp.bfloat16
MESH = pl.DeviceIdType.MESH

SIDES = ((0, -1), (0, 1), (-1, 0), (1, 0), (-1, -1), (-1, 1), (1, -1), (1, 1))
OPPOSITE = (1, 0, 3, 2, 7, 6, 5, 4)
OFFSET = (0, 40, 80, 112, 144, 160, 176, 192)
COUNT = (40, 40, 32, 32, 16, 16, 16, 16)
RIM = 208
LINE_COUNT = (25, 25, 13, 13, 1, 1, 1, 1)
NEAR_COUNT = (31, 31, 19, 19, 7, 7, 7, 7)
FULL_COUNT = (37, 37, 25, 25, 13, 13, 13, 13)
DIRECT = (2, 3, 0, 1)
DIAGONAL = (4, 5, 6, 7)
TURN_ROWS = (32, 32, 24, 24)
TURN_OFFSET = (0, 32, 64, 88)
TURN_RIM = 112
LINES = (
    (0, 25, 0, 16), (40, 25, 12, 16), (80, 13, 0, 1), (112, 13, 384, 1),
    (144, 1, 0, 1), (160, 1, 12, 1), (176, 1, 384, 1), (192, 1, 396, 1),
)
NEAR = (
    (25, 3, 1, 1), (28, 3, 385, 1), (65, 3, 9, 1), (68, 3, 393, 1),
    (93, 3, 16, 16), (96, 3, 28, 16), (125, 3, 336, 16), (128, 3, 348, 16),
    (145, 3, 1, 1), (148, 3, 16, 16), (161, 3, 9, 1), (164, 3, 28, 16),
    (177, 3, 385, 1), (180, 3, 336, 16), (193, 3, 393, 1), (196, 3, 348, 16),
)
FAR = (
    (31, 3, 4, 1), (34, 3, 388, 1), (71, 3, 6, 1), (74, 3, 390, 1),
    (99, 3, 64, 16), (102, 3, 76, 16), (131, 3, 288, 16), (134, 3, 300, 16),
    (151, 3, 4, 1), (154, 3, 64, 16), (167, 3, 6, 1), (170, 3, 76, 16),
    (183, 3, 388, 1), (186, 3, 288, 16), (199, 3, 390, 1), (202, 3, 300, 16),
)
SIDE_LINES = ((0, 25, 0, 16), (32, 25, 12, 16), (64, 13, 0, 1), (88, 13, 384, 1))
CORNER_LINES = LINES[4:]
PLACE, KNOWN, LINE, UNIQUE, CLOSE, SLOT, FACING = range(7)


def rim_tables():
    node = np.full(RIM, -1)
    line = np.zeros(RIM)
    close = np.zeros(RIM)
    for group in (LINES, NEAR, FAR):
        for first, rows, start, stride in group:
            node[first : first + rows] = start + stride * np.arange(rows)
            line[first : first + rows] = group is LINES
            close[first : first + rows] = group is not FAR
    place = np.arange(RIM) - 4000.0
    slot = np.zeros(RIM)
    lane_node = np.full(RIM, -1)
    for k in range(8):
        mine = np.arange(OFFSET[k], OFFSET[k] + COUNT[k])
        theirs = mine - OFFSET[k] + OFFSET[OPPOSITE[k]]
        slot[mine] = k
        lane_node[mine] = node[theirs]
        known = node[theirs] >= 0
        ny = node[theirs] // PITCH + 3 * TY * SIDES[k][0]
        nx = node[theirs] % PITCH + 3 * TX * SIDES[k][1]
        place[mine[known]] = ((ny + 8) * 64 + nx + 8)[known]
    facing = np.array(OPPOSITE)[slot.astype(int)]
    corner = np.zeros(RIM)
    corner[[0, 24, 40, 64, 80, 92, 112, 124]] = 1
    unique = line * (slot < 4) * np.where(slot < 2, 1, 1 - corner)
    rows = np.zeros((RIM, LEV))
    for column, table in enumerate((place, node >= 0, line, unique, close, slot, facing)):
        rows[:, column] = table
    lanes = np.full((3, 8, 2 * LEV), -9000.0)
    lanes[:, :, :RIM] = np.stack([lane_node, place, slot])[:, None]
    return rows.astype(np.float32), lanes.astype(np.float32)


def iota(shape, dim):
    return lax.broadcasted_iota(jnp.int32, shape, dim)


def halves(x):
    high = x.astype(BF16)
    return high, (x - high.astype(F32)).astype(BF16)


def stack2(x):
    high, low = halves(x)
    return jnp.concatenate([high, low], axis=0)


def stack3(x):
    high, low = halves(x)
    return jnp.concatenate([high, low, high], axis=0)


def weight3(x):
    high, low = halves(x)
    return jnp.where(iota(x.shape, 1) < 2 * (x.shape[1] // 3), high.astype(F32), low.astype(F32)).astype(BF16)


def mm(a, b):
    return jnp.dot(a, b, preferred_element_type=F32)


def exact(a, b):
    return jnp.dot(a, b, preferred_element_type=F32, precision=lax.Precision.HIGHEST)


def onehot(cond):
    return jnp.where(cond, 1.0, 0.0).astype(F32)


def block_diag(matrix, cols):
    left = onehot(iota((STRIP, 16), 0) % 16 == iota((STRIP, 16), 1))
    right = onehot(iota((16, cols), 1) % 16 == iota((16, cols), 0))
    spread = exact(exact(left, matrix), right)
    same = (iota((STRIP, cols), 1) % STRIP) // 16 == iota((STRIP, cols), 0) // 16
    return jnp.where(same, spread, 0.0)


def node_point(node, point):
    return (node // PITCH == (point % 16) // 4) & (node % PITCH == 3 * (point // 16) + point % 4)


def gather_rim(grid, send, groups, blocks, first=0):
    for n, k in enumerate(blocks):
        for group in groups:
            for row, rows, start, stride in group:
                send[first + n, row : row + rows] = grid[k, pl.ds(start, rows, stride=stride)]


def add_rim(grid, recv, blocks, lines=LINES):
    for k in blocks:
        for row, rows, start, stride in lines:
            nodes = pl.ds(start, rows, stride=stride)
            grid[k, nodes] = grid[k, nodes] + recv[k, row : row + rows]


def lanes_of(ref, blocks):
    return jnp.concatenate([ref[k] for k in blocks], axis=1)


def spread_rows(parts):
    filled = []
    for k, part in enumerate(parts):
        filled.append(part)
        if part.shape[0] < COUNT[k]:
            filled.append(jnp.zeros((COUNT[k] - part.shape[0], part.shape[1]), F32))
    return jnp.concatenate(filled, axis=0)


def swap_sides(x):
    return jnp.concatenate([x[OFFSET[k] : OFFSET[k] + COUNT[k]] for k in OPPOSITE], axis=0)


def mm3(weight, x):
    w_high, w_low = weight if isinstance(weight, tuple) else halves(weight[:, :RIM])
    high, low = halves(x)
    return mm(w_high, high) + mm(w_high, low) + mm(w_low, high)


def step_kernel(
    pot_in, tracer_in, u_in, v_in, w_in, geo_in, mass_hbm, dx_hbm, dy_hbm, col_hbm, cells_hbm, row_hbm, lane_hbm,
    out,
    mass_in, dx_in, dy_in, col_in, cells, cells_row, row_tab, lane_tab,
    xin, xc, mid, s1, s2, s3, s4, mgrid, rinv, mcol, kmat, inv,
    send1, recv0, recv1, recv_vert, local, packed, away, foreign, rim_inv,
    load_sem, send_sem, recv_sem,
):
    row = lax.axis_index("sfc")
    col = lax.axis_index("sub")
    n_row = lax.axis_size("sfc")
    n_col = lax.axis_size("sub")

    def device(side):
        return (lax.rem(row + side[0] + n_row, n_row), lax.rem(col + side[1] + n_col, n_col))

    barrier = pltpu.get_barrier_semaphore()
    for side in SIDES:
        pl.semaphore_signal(barrier, inc=1, device_id=device(side), device_id_type=MESH)

    sources = (geo_in, w_in, pot_in, tracer_in, u_in, v_in)
    loads = [pltpu.make_async_copy(ref, xin.at[k], load_sem.at[k]) for k, ref in enumerate(sources)]
    smalls = [
        pltpu.make_async_copy(source, place, load_sem.at[FIELDS + k])
        for k, (source, place) in enumerate(
            (
                (cells_hbm, cells), (cells_hbm, cells_row), (mass_hbm, mass_in), (dx_hbm, dx_in), (dy_hbm, dy_in),
                (col_hbm, col_in), (row_hbm, row_tab), (lane_hbm, lane_tab),
            )
        )
    ]
    for load in smalls + loads:
        load.start()

    def exchange(turn, send, recv, sides, start, counts, blocks=None, land=None):
        copies = []
        for k in sides:
            source, target = start[k], (land or start)[OPPOSITE[k]]
            lanes = pl.ds(0, send.shape[0]) if blocks is None else pl.ds(*blocks)
            copies.append(
                pltpu.make_async_remote_copy(
                    src_ref=send.at[lanes, pl.ds(source, counts[k])],
                    dst_ref=recv.at[lanes, pl.ds(target, counts[k])],
                    send_sem=send_sem.at[turn, k],
                    recv_sem=recv_sem.at[turn, OPPOSITE[k]],
                    device_id=device(SIDES[k]),
                    device_id_type=MESH,
                )
            )
        for copy in copies:
            copy.start()
        return copies

    for load in smalls:
        load.wait()

    def invert(c, carry):
        slot = jnp.int32(0)
        for j in range(TX * TY):
            slot = jnp.where(cells[0, j] == c, j, slot)
        inv[c] = slot
        return carry

    lax.fori_loop(0, TX * TY, invert, 0, unroll=True)

    dx = dx_in[...]
    dy = dy_in[...]
    deriv3 = weight3(jnp.concatenate([block_diag(dx, 3 * STRIP), block_diag(dy, 3 * STRIP)], axis=0))
    gather2 = onehot(node_point(iota((STRIP, 2 * STRIP), 0), iota((STRIP, 2 * STRIP), 1) % STRIP)).astype(BF16)
    spread2 = onehot(node_point(iota((STRIP, 2 * STRIP), 1) % STRIP, iota((STRIP, 2 * STRIP), 0))).astype(BF16)

    for send in (send1, local):
        send[...] = jnp.zeros_like(send)
    for grid in (s1, s2, s3, s4, mgrid):
        grid[:, 0:16] = jnp.zeros((grid.shape[0], 16, LEV), F32)

    def accumulate(grid, start, vals):
        head = pl.ds(start, 16)
        tail = pl.ds(pl.multiple_of(start + 16, 16), STRIP - 16)
        for k in range(grid.shape[0]):
            part = vals[:, k * LEV : (k + 1) * LEV]
            grid[k, head] = grid[k, head] + part[0:16]
            grid[k, tail] = part[16:]

    def scaled_strip(grid, here, inverse, count):
        return jnp.concatenate([grid[k, here] * inverse for k in range(count)], axis=1)

    def mass_strip(ey, carry):
        points = []
        for ex in range(TX):
            chosen = jnp.where(cells_row[...] == TX * ey + ex, mass_in[...], 0.0)
            points.append(jnp.broadcast_to(jnp.sum(chosen, axis=1, keepdims=True), (16, LEV)))
        strip_mass = jnp.concatenate(points, axis=0)
        mcol[pl.ds(pl.multiple_of(STRIP * ey, STRIP), STRIP)] = strip_mass
        accumulate(mgrid, pl.multiple_of(48 * ey, 16), mm(gather2, stack2(strip_mass)))
        return carry

    lax.fori_loop(0, TY, mass_strip, 0, unroll=True)
    gather_rim(mgrid, send1, (LINES, NEAR, FAR), range(1), 1)
    lap = exact(dx, dx) + exact(dy, dy)
    lap_blk = block_diag(lap, 3 * STRIP)
    spread3 = onehot(node_point(iota((STRIP, 3 * STRIP), 1) % STRIP, iota((STRIP, 3 * STRIP), 0)))
    lap_nodes = exact(block_diag(lap, STRIP), spread3)

    def matrix_strip(ey, carry):
        strip_mass = mcol[pl.ds(pl.multiple_of(STRIP * ey, STRIP), STRIP)]
        wide = jnp.concatenate([strip_mass, strip_mass[:, :STRIP]], axis=1)
        kmat[0, ey] = weight3(mm(gather2, stack2(wide * lap_blk)))
        kmat[1, ey] = weight3(mm(gather2, stack2(wide * lap_nodes)))
        return carry

    lax.fori_loop(0, TY, matrix_strip, 0, unroll=True)

    for load in loads:
        load.wait()

    def strip_of(ref, ey, fields):
        return jnp.concatenate([ref[k, pl.ds(TX * ey, TX)].reshape(STRIP, LEV) for k in fields], axis=1)

    def tend_strip(ey, carry):
        points = pl.ds(pl.multiple_of(STRIP * ey, STRIP), STRIP)
        fields = []
        for k in range(FIELDS):
            parts = [xin[k, inv[TX * ey + ex]] for ex in range(TX)]
            for ex in range(TX):
                xc[k, TX * ey + ex] = parts[ex]
            fields.append(jnp.concatenate(parts, axis=0))
        x = jnp.concatenate(fields, axis=1)
        slopes = mm(deriv3, stack3(x[:, : 4 * LEV]))
        sx = slopes[:STRIP]
        sy = slopes[STRIP:]
        pot = x[:, 2 * LEV : 3 * LEV]
        u = x[:, 4 * LEV : 5 * LEV]
        v = x[:, 5 * LEV : 6 * LEV]

        def advect(k):
            cols = slice(k * LEV, (k + 1) * LEV)
            return -(u * sx[:, cols] + v * sy[:, cols])

        tend = [advect(2), advect(3), -sx[:, :LEV], -sy[:, :LEV], advect(1) + buoyancy * pot]
        weight = mcol[points]
        weighted = jnp.concatenate([t * weight for t in tend], axis=1)
        start = pl.multiple_of(48 * ey, 16)
        accumulate(s1, start, mm(gather2, stack2(weighted)))
        return carry

    lax.fori_loop(0, TY, tend_strip, 0, unroll=True)
    gather_rim(s1, send1, (LINES,), range(4, 5), 0)
    gather_rim(s1, send1, (LINES, NEAR, FAR), range(4), 2)
    pl.semaphore_wait(barrier, 8)
    far_start = [first + n for first, n in zip(OFFSET, LINE_COUNT)]
    far_count = [n - m for m, n in zip(LINE_COUNT, FULL_COUNT)]
    vert_copies = exchange(4, send1, recv_vert, range(8), OFFSET, LINE_COUNT, (0, 2))
    line_copies = exchange(0, send1, recv0, DIRECT, OFFSET, LINE_COUNT, (2, 4), TURN_OFFSET)
    line_copies += exchange(1, send1, recv1, DIAGONAL, OFFSET, FULL_COUNT, (1, 5))
    line_copies += exchange(2, send1, recv1, DIRECT, far_start, far_count, (1, 5))

    col_high, col_low = halves(col_in[...])
    col3 = jnp.concatenate(
        [jnp.concatenate([col_high, col_low], axis=1), jnp.concatenate([col_high, jnp.zeros_like(col_low)], axis=1)],
        axis=0,
    )

    def newton(elements, which):
        change = {}
        for ey in sorted({ey for ey, _ in elements}):
            here = pl.ds(48 * ey, STRIP)
            change[ey] = mm(spread2, stack2(s1[4, here] * (rinv[which, here] * time_step)))
        for first in range(0, len(elements), 20):
            part = elements[first : first + 20]
            rows = [change[ey][16 * ex : 16 * ex + 16] + xc[1, TX * ey + ex] for ey, ex in part]
            geo = jnp.concatenate([xc[0, TX * ey + ex] for ey, ex in part], axis=0)
            target = geo + gravity_step * jnp.concatenate(rows, axis=0)
            phi = target
            lane = iota(phi.shape, 1)
            for _ in range(NEWTON):
                above = jnp.where(lane == LEV - 1, 0.0, pltpu.roll(phi, LEV - 1, 1))
                flux = jnp.tanh(above - phi)
                below = jnp.where(lane == 0, 0.0, pltpu.roll(flux, 1, 1))
                resid = phi - target - column_couple * (flux - below)
                step = mm(jnp.concatenate(halves(resid), axis=1), col3)
                phi = phi - (step[:, :LEV] + step[:, LEV:])
            for n, (ey, ex) in enumerate(part):
                mid[TX * ey + ex] = phi[16 * n : 16 * n + 16]

    def column(kind):
        return row_tab[:, kind : kind + 1]

    same_place = onehot(column(PLACE) == lane_tab[1][0:1, :RIM]).astype(BF16)

    def merge(x):
        high, low = halves(x)
        return mm(same_place, high) + mm(same_place, low)

    def reciprocal(total):
        return jnp.where(total > 0.0, 1.0 / jnp.where(total > 0.0, total, 1.0), 0.0)

    node_row = iota((NODES, LEV), 0) // PITCH
    node_col = iota((NODES, LEV), 0) % PITCH
    inside = (node_row > 0) & (node_row < ROWS - 1) & (node_col > 0) & (node_col < 12)
    rinv[1] = jnp.where(inside, reciprocal(mgrid[0]), 0.0)

    def first_strip(ey, carry):
        start = pl.multiple_of(48 * ey, 16)
        here = pl.ds(start, STRIP)
        rims = onehot((iota((STRIP, 2 * LEV), 0) + start).astype(F32) == lane_tab[0][0:1])
        nodal = jnp.concatenate([scaled_strip(s1, here, rinv[1, here] * time_step, 4), rims], axis=1)
        response = mm(kmat[1, ey], stack3(nodal))
        own = mm(kmat[0, ey], stack3(strip_of(xc, ey, (2, 3, 4, 5))))
        accumulate(s2, start, jnp.concatenate([response[:, : 4 * LEV] + own, response[:, 4 * LEV :]], axis=1))
        return carry

    lax.fori_loop(0, TY, first_strip, 0, unroll=True)
    gather_rim(s2, local, (LINES, NEAR), range(6))
    facing = column(FACING) == lane_tab[2][0:1]

    def fold(blocks):
        both = jnp.where(facing, lanes_of(local, blocks), 0.0)
        return both[:, :LEV] + both[:, LEV:]

    packed[0:4] = local[0:4]
    packed[4] = fold(range(4, 6))
    near_copies = exchange(3, packed, away, range(8), OFFSET, NEAR_COUNT, (0, 5))

    def second_strip(ey, carry):
        start = pl.multiple_of(48 * ey, 16)
        here = pl.ds(start, STRIP)
        accumulate(s3, start, mm(kmat[1, ey], stack3(scaled_strip(s2, here, rinv[1, here], 6))))
        return carry

    lax.fori_loop(0, TY, second_strip, 0, unroll=True)
    gather_rim(s3, local, (LINES,), range(6), 6)
    packed[5:9] = local[6:10]
    packed[9] = fold(range(10, 12))
    far_copies = exchange(5, packed, away, range(8), OFFSET, LINE_COUNT, (5, 5))

    own_weight = halves(lanes_of(local, range(4, 6))[:, :RIM])
    again_weight = halves(lanes_of(s3, range(4, 6))[:, :RIM])
    inner_weight = halves(lanes_of(s2, range(4, 6))[:, :RIM])
    newton([(ey, ex) for ey in range(1, TY - 1) for ex in (1, 2)], 1)

    def wide(x):
        return jnp.concatenate([x] * 4, axis=1)

    known = column(KNOWN) > 0.0
    line = column(LINE)
    unique = column(UNIQUE)
    side_line = (line > 0.0) & (column(SLOT) < 3.5)
    own_block = column(SLOT) == lane_tab[2][0:1]
    close = column(CLOSE) > 0.0

    for copy in vert_copies + line_copies + near_copies + far_copies:
        copy.wait_send()
    for copy in vert_copies:
        copy.wait_recv()
    add_rim(mgrid, recv_vert.at[pl.ds(1, 1)], range(1))
    rinv[0] = reciprocal(mgrid[0])
    for row, rows, start, stride in LINES:
        nodes = pl.ds(start, rows, stride=stride)
        s1[4, nodes] = s1[4, nodes] + recv_vert[0, row : row + rows]
    newton(
        [(ey, ex) for ey in range(1, TY - 1) for ex in (0, 3)] + [(ey, ex) for ey in (0, TY - 1) for ex in range(TX)], 0
    )

    for copy in line_copies:
        copy.wait_recv()
    side_lines = spread_rows(
        [lanes_of(recv0, range(2, 6))[first : first + rows] for first, rows in zip(TURN_OFFSET, TURN_ROWS)]
        + [jnp.zeros((16, 4 * LEV), F32)] * 4
    )
    arrived_all = jnp.where(side_line, side_lines, jnp.where(known, lanes_of(recv1, range(2, 6)), 0.0))
    mass_all = jnp.where(line > 0.0, recv_vert[1], jnp.where(known, recv1[1], 0.0))
    rim_inv[...] = reciprocal(merge(mass_all + unique * send1[1]))
    totals = merge(arrived_all + unique * lanes_of(send1, range(2, 6)))
    rim_state = totals * wide(rim_inv[...] * time_step)
    outer = swap_sides(unique * rim_state)
    for k in range(4):
        for row, rows, start, stride in SIDE_LINES:
            nodes = pl.ds(start, rows, stride=stride)
            s1[k, nodes] = s1[k, nodes] + recv0[2 + k, row : row + rows]
        for row, rows, start, stride in CORNER_LINES:
            nodes = pl.ds(start, rows, stride=stride)
            s1[k, nodes] = s1[k, nodes] + recv1[2 + k, row : row + rows]
    own_sum = lanes_of(local, range(4)) + mm3(own_weight, outer)
    own_rim = jnp.where(line > 0.0, own_sum, 0.0) * wide(rim_inv[...])
    again = lanes_of(s3, range(4)) + mm3(again_weight, outer)
    for k in range(4):
        s4[k] = again[:, k * LEV : (k + 1) * LEV]

    def place_column(j, carry):
        phi = mid[cells[0, j]]
        out[5, j] = phi
        out[4, j] = (phi - xc[0, cells[0, j]]) / gravity_step
        return carry

    lax.fori_loop(0, TX * TY, place_column, 0, unroll=True)

    inverse = rim_inv[...]
    for copy in near_copies:
        copy.wait_recv()
    rim_matrix = jnp.where(own_block & close, lanes_of(away, (4, 4)), 0.0)
    first_turn = jnp.where(close, lanes_of(away, range(4)), 0.0) + mm3(rim_matrix, rim_state)
    rim_next = merge(first_turn) * wide(inverse) + own_rim
    outside = mm3(rim_matrix, rim_next)
    inner = mm3(inner_weight, swap_sides(rim_next * unique))
    for copy in far_copies:
        copy.wait_recv()
    rim_matrix2 = jnp.where(own_block & (line > 0.0), lanes_of(away, (9, 9)), 0.0)
    outside = outside + jnp.where(line > 0.0, lanes_of(away, range(5, 9)), 0.0) + mm3(rim_matrix2, rim_state)
    for k in range(4):
        foreign[k] = outside[:, k * LEV : (k + 1) * LEV]
        s4[k] = s4[k] + inner[:, k * LEV : (k + 1) * LEV]
    add_rim(s4, foreign, range(4))

    def final_strip(ey, carry):
        here = pl.ds(pl.multiple_of(48 * ey, 16), STRIP)
        inverse = rinv[0, here]
        nodal = jnp.concatenate(
            [(time_step * s1[k, here] - visc_coef * s4[k, here]) * inverse for k in range(4)], axis=1
        )
        final = strip_of(xc, ey, (2, 3, 4, 5)) + mm(spread2, stack2(nodal))
        for k in range(4):
            xc[2 + k, pl.ds(TX * ey, TX)] = final[:, k * LEV : (k + 1) * LEV].reshape(TX, 16, LEV)
        return carry

    lax.fori_loop(0, TY, final_strip, 0, unroll=True)

    def place_fields(j, carry):
        for k in range(4):
            out[k, j] = xc[2 + k, cells[0, j]]
        return carry

    lax.fori_loop(0, TX * TY, place_fields, 0, unroll=True)


def store_kernel(fields, *refs):
    outs, sem = refs[:FIELDS], refs[FIELDS]
    copies = [pltpu.make_async_copy(fields.at[k], outs[k], sem.at[k]) for k in range(FIELDS)]
    for copy in copies:
        copy.start()
    for copy in copies:
        copy.wait()


def per_device(pot_temp, tracer, wind_u, wind_v, vert_w, geopot, elem_mass, deriv_x, deriv_y, col_inverse, element_cell):
    shape = pot_temp.shape
    vmem = pl.BlockSpec(memory_space=pltpu.VMEM)
    hbm = pl.BlockSpec(memory_space=pl.ANY)
    rows, lanes = rim_tables()
    fields = pl.pallas_call(
        step_kernel,
        out_shape=pltpu.VMEM((FIELDS,) + shape, F32),
        in_specs=[hbm] * 13,
        out_specs=vmem,
        scratch_shapes=[
            pltpu.VMEM((16, TX * TY), F32),
            pltpu.VMEM((16, 16), F32),
            pltpu.VMEM((16, 16), F32),
            pltpu.VMEM((LEV, LEV), F32),
            pltpu.SMEM((1, TX * TY), jnp.int32),
            pltpu.VMEM((1, TX * TY), jnp.int32),
            pltpu.VMEM(rows.shape, F32),
            pltpu.VMEM(lanes.shape, F32),
            pltpu.VMEM((FIELDS,) + shape, F32),
            pltpu.VMEM((FIELDS,) + shape, F32),
            pltpu.VMEM(shape, F32),
            pltpu.VMEM((5, NODES, LEV), F32),
            pltpu.VMEM((6, NODES, LEV), F32),
            pltpu.VMEM((6, NODES, LEV), F32),
            pltpu.VMEM((4, NODES, LEV), F32),
            pltpu.VMEM((1, NODES, LEV), F32),
            pltpu.VMEM((2, NODES, LEV), F32),
            pltpu.VMEM((512, LEV), F32),
            pltpu.VMEM((2, TY, STRIP, 3 * STRIP), BF16),
            pltpu.SMEM((TX * TY,), jnp.int32),
        ]
        + [pltpu.VMEM((6, RIM, LEV), F32), pltpu.VMEM((6, TURN_RIM, LEV), F32), pltpu.VMEM((6, RIM, LEV), F32)]
        + [pltpu.VMEM((2, RIM, LEV), F32)]
        + [pltpu.VMEM((blocks, RIM, LEV), F32) for blocks in (12, 10, 10, 4)]
        + [
            pltpu.VMEM((RIM, LEV), F32),
            pltpu.SemaphoreType.DMA((FIELDS + 8,)),
            pltpu.SemaphoreType.DMA((6, 8)),
            pltpu.SemaphoreType.DMA((6, 8)),
        ],
        compiler_params=pltpu.CompilerParams(collective_id=0, has_side_effects=True, vmem_limit_bytes=62 << 20),
    )(pot_temp, tracer, wind_u, wind_v, vert_w, geopot, elem_mass.T, deriv_x, deriv_y, col_inverse, element_cell, rows, lanes)
    result = jax.ShapeDtypeStruct(shape, F32)
    return tuple(
        pl.pallas_call(
            store_kernel,
            out_shape=[result] * FIELDS,
            in_specs=[vmem],
            out_specs=[hbm] * FIELDS,
            scratch_shapes=[pltpu.SemaphoreType.DMA((FIELDS,))],
            compiler_params=pltpu.CompilerParams(vmem_limit_bytes=48 << 20),
        )(fields)
    )


def solution(mesh):
    field = P(("sfc", "sub"), None, None)
    flat = P(("sfc", "sub"), None)
    return jax.shard_map(
        per_device,
        mesh=mesh,
        in_specs=(field,) * 6 + (flat, P(), P(), P(), flat),
        out_specs=(field,) * 6,
        check_vma=False,
    )
```

```python
import jax
import jax.numpy as jnp
import numpy as np
from jax import lax
from jax.experimental import pallas as pl
from jax.experimental.pallas import tpu as pltpu
from jax.sharding import PartitionSpec as P

TX = 4
TY = 8
LEV = 128
NEWTON = 3
PITCH = 16
ROWS = 3 * TY + 1
NODES = ROWS * PITCH
STRIP = 64
FIELDS = 6

time_step = 0.4
visc_coef = 0.1
buoyancy = 0.5
gravity_step = 0.5
column_couple = 0.25

F32 = jnp.float32
BF16 = jnp.bfloat16
MESH = pl.DeviceIdType.MESH

SIDES = ((0, -1), (0, 1), (-1, 0), (1, 0), (-1, -1), (-1, 1), (1, -1), (1, 1))
OPPOSITE = (1, 0, 3, 2, 7, 6, 5, 4)
OFFSET = (0, 40, 80, 112, 144, 160, 176, 192)
COUNT = (40, 40, 32, 32, 16, 16, 16, 16)
RIM = 208
LINE_COUNT = (25, 25, 13, 13, 1, 1, 1, 1)
NEAR_COUNT = (31, 31, 19, 19, 7, 7, 7, 7)
FULL_COUNT = (37, 37, 25, 25, 13, 13, 13, 13)
DIRECT = (2, 3, 0, 1)
DIAGONAL = (4, 5, 6, 7)
TURN_ROWS = (32, 32, 24, 24)
TURN_OFFSET = (0, 32, 64, 88)
TURN_RIM = 112
LINES = (
    (0, 25, 0, 16), (40, 25, 12, 16), (80, 13, 0, 1), (112, 13, 384, 1),
    (144, 1, 0, 1), (160, 1, 12, 1), (176, 1, 384, 1), (192, 1, 396, 1),
)
NEAR = (
    (25, 3, 1, 1), (28, 3, 385, 1), (65, 3, 9, 1), (68, 3, 393, 1),
    (93, 3, 16, 16), (96, 3, 28, 16), (125, 3, 336, 16), (128, 3, 348, 16),
    (145, 3, 1, 1), (148, 3, 16, 16), (161, 3, 9, 1), (164, 3, 28, 16),
    (177, 3, 385, 1), (180, 3, 336, 16), (193, 3, 393, 1), (196, 3, 348, 16),
)
FAR = (
    (31, 3, 4, 1), (34, 3, 388, 1), (71, 3, 6, 1), (74, 3, 390, 1),
    (99, 3, 64, 16), (102, 3, 76, 16), (131, 3, 288, 16), (134, 3, 300, 16),
    (151, 3, 4, 1), (154, 3, 64, 16), (167, 3, 6, 1), (170, 3, 76, 16),
    (183, 3, 388, 1), (186, 3, 288, 16), (199, 3, 390, 1), (202, 3, 300, 16),
)
SIDE_LINES = ((0, 25, 0, 16), (32, 25, 12, 16), (64, 13, 0, 1), (88, 13, 384, 1))
CORNER_LINES = LINES[4:]
PLACE, KNOWN, LINE, UNIQUE, CLOSE, SLOT, FACING = range(7)


def rim_tables():
    node = np.full(RIM, -1)
    line = np.zeros(RIM)
    close = np.zeros(RIM)
    for group in (LINES, NEAR, FAR):
        for first, rows, start, stride in group:
            node[first : first + rows] = start + stride * np.arange(rows)
            line[first : first + rows] = group is LINES
            close[first : first + rows] = group is not FAR
    place = np.arange(RIM) - 4000.0
    slot = np.zeros(RIM)
    lane_node = np.full(RIM, -1)
    for k in range(8):
        mine = np.arange(OFFSET[k], OFFSET[k] + COUNT[k])
        theirs = mine - OFFSET[k] + OFFSET[OPPOSITE[k]]
        slot[mine] = k
        lane_node[mine] = node[theirs]
        known = node[theirs] >= 0
        ny = node[theirs] // PITCH + 3 * TY * SIDES[k][0]
        nx = node[theirs] % PITCH + 3 * TX * SIDES[k][1]
        place[mine[known]] = ((ny + 8) * 64 + nx + 8)[known]
    facing = np.array(OPPOSITE)[slot.astype(int)]
    corner = np.zeros(RIM)
    corner[[0, 24, 40, 64, 80, 92, 112, 124]] = 1
    unique = line * (slot < 4) * np.where(slot < 2, 1, 1 - corner)
    rows = np.zeros((RIM, LEV))
    for column, table in enumerate((place, node >= 0, line, unique, close, slot, facing)):
        rows[:, column] = table
    lanes = np.full((3, 8, 2 * LEV), -9000.0)
    lanes[:, :, :RIM] = np.stack([lane_node, place, slot])[:, None]
    return rows.astype(np.float32), lanes.astype(np.float32)


def iota(shape, dim):
    return lax.broadcasted_iota(jnp.int32, shape, dim)


def halves(x):
    high = x.astype(BF16)
    return high, (x - high.astype(F32)).astype(BF16)


def stack2(x):
    high, low = halves(x)
    return jnp.concatenate([high, low], axis=0)


def stack3(x):
    high, low = halves(x)
    return jnp.concatenate([high, low, high], axis=0)


def weight3(x):
    high, low = halves(x)
    return jnp.where(iota(x.shape, 1) < 2 * (x.shape[1] // 3), high.astype(F32), low.astype(F32)).astype(BF16)


def mm(a, b):
    return jnp.dot(a, b, preferred_element_type=F32)


def exact(a, b):
    return jnp.dot(a, b, preferred_element_type=F32, precision=lax.Precision.HIGHEST)


def onehot(cond):
    return jnp.where(cond, 1.0, 0.0).astype(F32)


def block_diag(matrix, cols):
    left = onehot(iota((STRIP, 16), 0) % 16 == iota((STRIP, 16), 1))
    right = onehot(iota((16, cols), 1) % 16 == iota((16, cols), 0))
    spread = exact(exact(left, matrix), right)
    same = (iota((STRIP, cols), 1) % STRIP) // 16 == iota((STRIP, cols), 0) // 16
    return jnp.where(same, spread, 0.0)


def node_point(node, point):
    return (node // PITCH == (point % 16) // 4) & (node % PITCH == 3 * (point // 16) + point % 4)


def gather_rim(grid, send, groups, blocks, first=0):
    for n, k in enumerate(blocks):
        for group in groups:
            for row, rows, start, stride in group:
                send[first + n, row : row + rows] = grid[k, pl.ds(start, rows, stride=stride)]


def add_rim(grid, recv, blocks, lines=LINES):
    for k in blocks:
        for row, rows, start, stride in lines:
            nodes = pl.ds(start, rows, stride=stride)
            grid[k, nodes] = grid[k, nodes] + recv[k, row : row + rows]


def lanes_of(ref, blocks):
    return jnp.concatenate([ref[k] for k in blocks], axis=1)


def spread_rows(parts):
    filled = []
    for k, part in enumerate(parts):
        filled.append(part)
        if part.shape[0] < COUNT[k]:
            filled.append(jnp.zeros((COUNT[k] - part.shape[0], part.shape[1]), F32))
    return jnp.concatenate(filled, axis=0)


def swap_sides(x):
    return jnp.concatenate([x[OFFSET[k] : OFFSET[k] + COUNT[k]] for k in OPPOSITE], axis=0)


def mm3(weight, x):
    w_high, w_low = weight if isinstance(weight, tuple) else halves(weight[:, :RIM])
    high, low = halves(x)
    return mm(w_high, high) + mm(w_high, low) + mm(w_low, high)


def step_kernel(
    pot_in, tracer_in, u_in, v_in, w_in, geo_in, mass_hbm, dx_hbm, dy_hbm, col_hbm, cells_hbm, row_hbm, lane_hbm,
    out,
    mass_in, dx_in, dy_in, col_in, cells, cells_row, row_tab, lane_tab,
    xin, xc, mid, s1, s2, s3, s4, mgrid, rinv, mcol, kmat, inv,
    send1, recv0, recv1, recv_vert, local, away, foreign, rim_inv,
    load_sem, send_sem, recv_sem,
):
    row = lax.axis_index("sfc")
    col = lax.axis_index("sub")
    n_row = lax.axis_size("sfc")
    n_col = lax.axis_size("sub")

    def device(side):
        return (lax.rem(row + side[0] + n_row, n_row), lax.rem(col + side[1] + n_col, n_col))

    barrier = pltpu.get_barrier_semaphore()
    for side in SIDES:
        pl.semaphore_signal(barrier, inc=1, device_id=device(side), device_id_type=MESH)

    sources = (geo_in, w_in, pot_in, tracer_in, u_in, v_in)
    loads = [pltpu.make_async_copy(ref, xin.at[k], load_sem.at[k]) for k, ref in enumerate(sources)]
    smalls = [
        pltpu.make_async_copy(source, place, load_sem.at[FIELDS + k])
        for k, (source, place) in enumerate(
            (
                (cells_hbm, cells), (cells_hbm, cells_row), (mass_hbm, mass_in), (dx_hbm, dx_in), (dy_hbm, dy_in),
                (col_hbm, col_in), (row_hbm, row_tab), (lane_hbm, lane_tab),
            )
        )
    ]
    for load in smalls + loads:
        load.start()

    def exchange(turn, send, recv, sides, start, counts, blocks=None, land=None):
        copies = []
        for k in sides:
            source, target = start[k], (land or start)[OPPOSITE[k]]
            lanes = pl.ds(0, send.shape[0]) if blocks is None else pl.ds(*blocks)
            copies.append(
                pltpu.make_async_remote_copy(
                    src_ref=send.at[lanes, pl.ds(source, counts[k])],
                    dst_ref=recv.at[lanes, pl.ds(target, counts[k])],
                    send_sem=send_sem.at[turn, k],
                    recv_sem=recv_sem.at[turn, OPPOSITE[k]],
                    device_id=device(SIDES[k]),
                    device_id_type=MESH,
                )
            )
        for copy in copies:
            copy.start()
        return copies

    for load in smalls:
        load.wait()

    def invert(c, carry):
        slot = jnp.int32(0)
        for j in range(TX * TY):
            slot = jnp.where(cells[0, j] == c, j, slot)
        inv[c] = slot
        return carry

    lax.fori_loop(0, TX * TY, invert, 0, unroll=True)

    dx = dx_in[...]
    dy = dy_in[...]
    deriv3 = weight3(jnp.concatenate([block_diag(dx, 3 * STRIP), block_diag(dy, 3 * STRIP)], axis=0))
    gather2 = onehot(node_point(iota((STRIP, 2 * STRIP), 0), iota((STRIP, 2 * STRIP), 1) % STRIP)).astype(BF16)
    spread2 = onehot(node_point(iota((STRIP, 2 * STRIP), 1) % STRIP, iota((STRIP, 2 * STRIP), 0))).astype(BF16)

    for send in (send1, local):
        send[...] = jnp.zeros_like(send)
    for grid in (s1, s2, s3, s4, mgrid):
        grid[:, 0:16] = jnp.zeros((grid.shape[0], 16, LEV), F32)

    def accumulate(grid, start, vals):
        head = pl.ds(start, 16)
        tail = pl.ds(pl.multiple_of(start + 16, 16), STRIP - 16)
        for k in range(grid.shape[0]):
            part = vals[:, k * LEV : (k + 1) * LEV]
            grid[k, head] = grid[k, head] + part[0:16]
            grid[k, tail] = part[16:]

    def scaled_strip(grid, here, inverse, count):
        return jnp.concatenate([grid[k, here] * inverse for k in range(count)], axis=1)

    def mass_strip(ey, carry):
        points = []
        for ex in range(TX):
            chosen = jnp.where(cells_row[...] == TX * ey + ex, mass_in[...], 0.0)
            points.append(jnp.broadcast_to(jnp.sum(chosen, axis=1, keepdims=True), (16, LEV)))
        strip_mass = jnp.concatenate(points, axis=0)
        mcol[pl.ds(pl.multiple_of(STRIP * ey, STRIP), STRIP)] = strip_mass
        accumulate(mgrid, pl.multiple_of(48 * ey, 16), mm(gather2, stack2(strip_mass)))
        return carry

    lax.fori_loop(0, TY, mass_strip, 0, unroll=True)
    gather_rim(mgrid, send1, (LINES, NEAR, FAR), range(1), 1)
    lap = exact(dx, dx) + exact(dy, dy)
    lap_blk = block_diag(lap, 3 * STRIP)
    spread3 = onehot(node_point(iota((STRIP, 3 * STRIP), 1) % STRIP, iota((STRIP, 3 * STRIP), 0)))
    lap_nodes = exact(block_diag(lap, STRIP), spread3)

    def matrix_strip(ey, carry):
        strip_mass = mcol[pl.ds(pl.multiple_of(STRIP * ey, STRIP), STRIP)]
        wide = jnp.concatenate([strip_mass, strip_mass[:, :STRIP]], axis=1)
        kmat[0, ey] = weight3(mm(gather2, stack2(wide * lap_blk)))
        kmat[1, ey] = weight3(mm(gather2, stack2(wide * lap_nodes)))
        return carry

    lax.fori_loop(0, TY, matrix_strip, 0, unroll=True)

    for load in loads:
        load.wait()

    def strip_of(ref, ey, fields):
        return jnp.concatenate([ref[k, pl.ds(TX * ey, TX)].reshape(STRIP, LEV) for k in fields], axis=1)

    def tend_strip(ey, carry):
        points = pl.ds(pl.multiple_of(STRIP * ey, STRIP), STRIP)
        fields = []
        for k in range(FIELDS):
            parts = [xin[k, inv[TX * ey + ex]] for ex in range(TX)]
            for ex in range(TX):
                xc[k, TX * ey + ex] = parts[ex]
            fields.append(jnp.concatenate(parts, axis=0))
        x = jnp.concatenate(fields, axis=1)
        slopes = mm(deriv3, stack3(x[:, : 4 * LEV]))
        sx = slopes[:STRIP]
        sy = slopes[STRIP:]
        pot = x[:, 2 * LEV : 3 * LEV]
        u = x[:, 4 * LEV : 5 * LEV]
        v = x[:, 5 * LEV : 6 * LEV]

        def advect(k):
            cols = slice(k * LEV, (k + 1) * LEV)
            return -(u * sx[:, cols] + v * sy[:, cols])

        tend = [advect(2), advect(3), -sx[:, :LEV], -sy[:, :LEV], advect(1) + buoyancy * pot]
        weight = mcol[points]
        weighted = jnp.concatenate([t * weight for t in tend], axis=1)
        start = pl.multiple_of(48 * ey, 16)
        accumulate(s1, start, mm(gather2, stack2(weighted)))
        return carry

    lax.fori_loop(0, TY, tend_strip, 0, unroll=True)
    gather_rim(s1, send1, (LINES,), range(4, 5), 0)
    gather_rim(s1, send1, (LINES, NEAR, FAR), range(4), 2)
    pl.semaphore_wait(barrier, 8)
    far_start = [first + n for first, n in zip(OFFSET, LINE_COUNT)]
    far_count = [n - m for m, n in zip(LINE_COUNT, FULL_COUNT)]
    vert_copies = exchange(4, send1, recv_vert, (2, 3, 4, 5, 6, 7, 0, 1), OFFSET, LINE_COUNT, (0, 2))
    line_copies = exchange(1, send1, recv1, DIAGONAL, OFFSET, FULL_COUNT, (1, 5))
    line_copies += exchange(0, send1, recv0, DIRECT, OFFSET, LINE_COUNT, (2, 4), TURN_OFFSET)
    line_copies += exchange(2, send1, recv1, DIRECT, far_start, far_count, (1, 5))

    col_high, col_low = halves(col_in[...])
    col3 = jnp.concatenate(
        [jnp.concatenate([col_high, col_low], axis=1), jnp.concatenate([col_high, jnp.zeros_like(col_low)], axis=1)],
        axis=0,
    )

    def newton(elements, which):
        change = {}
        for ey in sorted({ey for ey, _ in elements}):
            here = pl.ds(48 * ey, STRIP)
            change[ey] = mm(spread2, stack2(s1[4, here] * (rinv[which, here] * time_step)))
        for first in range(0, len(elements), 20):
            part = elements[first : first + 20]
            rows = [change[ey][16 * ex : 16 * ex + 16] + xc[1, TX * ey + ex] for ey, ex in part]
            geo = jnp.concatenate([xc[0, TX * ey + ex] for ey, ex in part], axis=0)
            target = geo + gravity_step * jnp.concatenate(rows, axis=0)
            phi = target
            lane = iota(phi.shape, 1)
            for _ in range(NEWTON):
                above = jnp.where(lane == LEV - 1, 0.0, pltpu.roll(phi, LEV - 1, 1))
                flux = jnp.tanh(above - phi)
                below = jnp.where(lane == 0, 0.0, pltpu.roll(flux, 1, 1))
                resid = phi - target - column_couple * (flux - below)
                step = mm(jnp.concatenate(halves(resid), axis=1), col3)
                phi = phi - (step[:, :LEV] + step[:, LEV:])
            for n, (ey, ex) in enumerate(part):
                mid[TX * ey + ex] = phi[16 * n : 16 * n + 16]

    def column(kind):
        return row_tab[:, kind : kind + 1]

    same_place = onehot(column(PLACE) == lane_tab[1][0:1, :RIM]).astype(BF16)

    def merge(x):
        high, low = halves(x)
        return mm(same_place, high) + mm(same_place, low)

    def reciprocal(total):
        return jnp.where(total > 0.0, 1.0 / jnp.where(total > 0.0, total, 1.0), 0.0)

    node_row = iota((NODES, LEV), 0) // PITCH
    node_col = iota((NODES, LEV), 0) % PITCH
    inside = (node_row > 0) & (node_row < ROWS - 1) & (node_col > 0) & (node_col < 12)
    rinv[1] = jnp.where(inside, reciprocal(mgrid[0]), 0.0)

    def first_strip(ey, carry):
        start = pl.multiple_of(48 * ey, 16)
        here = pl.ds(start, STRIP)
        rims = onehot((iota((STRIP, 2 * LEV), 0) + start).astype(F32) == lane_tab[0][0:1])
        nodal = jnp.concatenate([scaled_strip(s1, here, rinv[1, here] * time_step, 4), rims], axis=1)
        response = mm(kmat[1, ey], stack3(nodal))
        own = mm(kmat[0, ey], stack3(strip_of(xc, ey, (2, 3, 4, 5))))
        accumulate(s2, start, jnp.concatenate([response[:, : 4 * LEV] + own, response[:, 4 * LEV :]], axis=1))
        return carry

    lax.fori_loop(0, TY, first_strip, 0, unroll=True)
    gather_rim(s2, local, (LINES, NEAR), range(4))
    gather_rim(s2, local, (LINES, NEAR), range(4, 6), 10)
    facing = column(FACING) == lane_tab[2][0:1]

    def fold(blocks):
        both = jnp.where(facing, lanes_of(local, blocks), 0.0)
        return both[:, :LEV] + both[:, LEV:]

    local[4] = fold(range(10, 12))
    near_copies = exchange(3, local, away, (2, 3, 4, 5, 6, 7, 0, 1), OFFSET, NEAR_COUNT, (0, 5))

    def second_strip(ey, carry):
        start = pl.multiple_of(48 * ey, 16)
        here = pl.ds(start, STRIP)
        accumulate(s3, start, mm(kmat[1, ey], stack3(scaled_strip(s2, here, rinv[1, here], 6))))
        return carry

    lax.fori_loop(0, TY, second_strip, 0, unroll=True)
    gather_rim(s3, local, (LINES,), range(4), 5)
    gather_rim(s3, local, (LINES,), range(4, 6), 12)
    local[9] = fold(range(12, 14))
    far_copies = exchange(5, local, away, (2, 3, 4, 5, 6, 7, 0, 1), OFFSET, LINE_COUNT, (5, 5))

    own_weight = halves(lanes_of(local, range(10, 12))[:, :RIM])
    again_weight = halves(lanes_of(s3, range(4, 6))[:, :RIM])
    inner_weight = halves(lanes_of(s2, range(4, 6))[:, :RIM])
    newton([(ey, ex) for ey in range(1, TY - 1) for ex in (1, 2)], 1)

    def wide(x):
        return jnp.concatenate([x] * 4, axis=1)

    known = column(KNOWN) > 0.0
    line = column(LINE)
    unique = column(UNIQUE)
    side_line = (line > 0.0) & (column(SLOT) < 3.5)
    own_block = column(SLOT) == lane_tab[2][0:1]
    close = column(CLOSE) > 0.0

    for copy in vert_copies + line_copies + near_copies + far_copies:
        copy.wait_send()
    for copy in vert_copies:
        copy.wait_recv()
    add_rim(mgrid, recv_vert.at[pl.ds(1, 1)], range(1))
    rinv[0] = reciprocal(mgrid[0])
    for row, rows, start, stride in LINES:
        nodes = pl.ds(start, rows, stride=stride)
        s1[4, nodes] = s1[4, nodes] + recv_vert[0, row : row + rows]
    newton(
        [(ey, ex) for ey in range(1, TY - 1) for ex in (0, 3)] + [(ey, ex) for ey in (0, TY - 1) for ex in range(TX)], 0
    )

    for copy in line_copies:
        copy.wait_recv()
    side_lines = spread_rows(
        [lanes_of(recv0, range(2, 6))[first : first + rows] for first, rows in zip(TURN_OFFSET, TURN_ROWS)]
        + [jnp.zeros((16, 4 * LEV), F32)] * 4
    )
    arrived_all = jnp.where(side_line, side_lines, jnp.where(known, lanes_of(recv1, range(2, 6)), 0.0))
    mass_all = jnp.where(line > 0.0, recv_vert[1], jnp.where(known, recv1[1], 0.0))
    rim_inv[...] = reciprocal(merge(mass_all + unique * send1[1]))
    totals = merge(arrived_all + unique * lanes_of(send1, range(2, 6)))
    rim_state = totals * wide(rim_inv[...] * time_step)
    outer = swap_sides(unique * rim_state)
    for k in range(4):
        for row, rows, start, stride in SIDE_LINES:
            nodes = pl.ds(start, rows, stride=stride)
            s1[k, nodes] = s1[k, nodes] + recv0[2 + k, row : row + rows]
        for row, rows, start, stride in CORNER_LINES:
            nodes = pl.ds(start, rows, stride=stride)
            s1[k, nodes] = s1[k, nodes] + recv1[2 + k, row : row + rows]
    own_sum = lanes_of(local, range(4)) + mm3(own_weight, outer)
    own_rim = jnp.where(line > 0.0, own_sum, 0.0) * wide(rim_inv[...])
    again = lanes_of(s3, range(4)) + mm3(again_weight, outer)
    for k in range(4):
        s4[k] = again[:, k * LEV : (k + 1) * LEV]

    def place_column(j, carry):
        phi = mid[cells[0, j]]
        out[5, j] = phi
        out[4, j] = (phi - xc[0, cells[0, j]]) / gravity_step
        return carry

    lax.fori_loop(0, TX * TY, place_column, 0, unroll=True)

    inverse = rim_inv[...]
    for copy in near_copies:
        copy.wait_recv()
    rim_matrix = jnp.where(own_block & close, lanes_of(away, (4, 4)), 0.0)
    first_turn = jnp.where(close, lanes_of(away, range(4)), 0.0) + mm3(rim_matrix, rim_state)
    rim_next = merge(first_turn) * wide(inverse) + own_rim
    outside = mm3(rim_matrix, rim_next)
    inner = mm3(inner_weight, swap_sides(rim_next * unique))
    for copy in far_copies:
        copy.wait_recv()
    rim_matrix2 = jnp.where(own_block & (line > 0.0), lanes_of(away, (9, 9)), 0.0)
    outside = outside + jnp.where(line > 0.0, lanes_of(away, range(5, 9)), 0.0) + mm3(rim_matrix2, rim_state)
    for k in range(4):
        foreign[k] = outside[:, k * LEV : (k + 1) * LEV]
        s4[k] = s4[k] + inner[:, k * LEV : (k + 1) * LEV]
    add_rim(s4, foreign, range(4))

    def final_strip(ey, carry):
        here = pl.ds(pl.multiple_of(48 * ey, 16), STRIP)
        inverse = rinv[0, here]
        nodal = jnp.concatenate(
            [(time_step * s1[k, here] - visc_coef * s4[k, here]) * inverse for k in range(4)], axis=1
        )
        final = strip_of(xc, ey, (2, 3, 4, 5)) + mm(spread2, stack2(nodal))
        for k in range(4):
            xc[2 + k, pl.ds(TX * ey, TX)] = final[:, k * LEV : (k + 1) * LEV].reshape(TX, 16, LEV)
        return carry

    lax.fori_loop(0, TY, final_strip, 0, unroll=True)

    def place_fields(j, carry):
        for k in range(4):
            out[k, j] = xc[2 + k, cells[0, j]]
        return carry

    lax.fori_loop(0, TX * TY, place_fields, 0, unroll=True)


def store_kernel(fields, *refs):
    outs, sem = refs[:FIELDS], refs[FIELDS]
    copies = [pltpu.make_async_copy(fields.at[k], outs[k], sem.at[k]) for k in range(FIELDS)]
    for copy in copies:
        copy.start()
    for copy in copies:
        copy.wait()


def per_device(pot_temp, tracer, wind_u, wind_v, vert_w, geopot, elem_mass, deriv_x, deriv_y, col_inverse, element_cell):
    shape = pot_temp.shape
    vmem = pl.BlockSpec(memory_space=pltpu.VMEM)
    hbm = pl.BlockSpec(memory_space=pl.ANY)
    rows, lanes = rim_tables()
    fields = pl.pallas_call(
        step_kernel,
        out_shape=pltpu.VMEM((FIELDS,) + shape, F32),
        in_specs=[hbm] * 13,
        out_specs=vmem,
        scratch_shapes=[
            pltpu.VMEM((16, TX * TY), F32),
            pltpu.VMEM((16, 16), F32),
            pltpu.VMEM((16, 16), F32),
            pltpu.VMEM((LEV, LEV), F32),
            pltpu.SMEM((1, TX * TY), jnp.int32),
            pltpu.VMEM((1, TX * TY), jnp.int32),
            pltpu.VMEM(rows.shape, F32),
            pltpu.VMEM(lanes.shape, F32),
            pltpu.VMEM((FIELDS,) + shape, F32),
            pltpu.VMEM((FIELDS,) + shape, F32),
            pltpu.VMEM(shape, F32),
            pltpu.VMEM((5, NODES, LEV), F32),
            pltpu.VMEM((6, NODES, LEV), F32),
            pltpu.VMEM((6, NODES, LEV), F32),
            pltpu.VMEM((4, NODES, LEV), F32),
            pltpu.VMEM((1, NODES, LEV), F32),
            pltpu.VMEM((2, NODES, LEV), F32),
            pltpu.VMEM((512, LEV), F32),
            pltpu.VMEM((2, TY, STRIP, 3 * STRIP), BF16),
            pltpu.SMEM((TX * TY,), jnp.int32),
        ]
        + [pltpu.VMEM((6, RIM, LEV), F32), pltpu.VMEM((6, TURN_RIM, LEV), F32), pltpu.VMEM((6, RIM, LEV), F32)]
        + [pltpu.VMEM((2, RIM, LEV), F32)]
        + [pltpu.VMEM((blocks, RIM, LEV), F32) for blocks in (14, 10, 4)]
        + [
            pltpu.VMEM((RIM, LEV), F32),
            pltpu.SemaphoreType.DMA((FIELDS + 8,)),
            pltpu.SemaphoreType.DMA((6, 8)),
            pltpu.SemaphoreType.DMA((6, 8)),
        ],
        compiler_params=pltpu.CompilerParams(collective_id=0, has_side_effects=True, vmem_limit_bytes=62 << 20),
    )(pot_temp, tracer, wind_u, wind_v, vert_w, geopot, elem_mass.T, deriv_x, deriv_y, col_inverse, element_cell, rows, lanes)
    result = jax.ShapeDtypeStruct(shape, F32)
    return tuple(
        pl.pallas_call(
            store_kernel,
            out_shape=[result] * FIELDS,
            in_specs=[vmem],
            out_specs=[hbm] * FIELDS,
            scratch_shapes=[pltpu.SemaphoreType.DMA((FIELDS,))],
            compiler_params=pltpu.CompilerParams(vmem_limit_bytes=48 << 20),
        )(fields)
    )


def solution(mesh):
    field = P(("sfc", "sub"), None, None)
    flat = P(("sfc", "sub"), None)
    return jax.shard_map(
        per_device,
        mesh=mesh,
        in_specs=(field,) * 6 + (flat, P(), P(), P(), flat),
        out_specs=(field,) * 6,
        check_vma=False,
    )
```
